512 devices in a mesh: dp: 32 (over y_lo, z), mp: 16 (over y_hi, x, core).
Axes of the slice: x: 4, y: 4 (y_hi: 2, y_lo: 2; y = y_hi * 2 + y_lo), z: 16, core: 2. Of those that a mesh axis runs over, the one named last changes fastest.
Arguments:
- queries_raw: bfloat16 [24576, 4096], P('dp', 'mp'), may hold values from -6 to 6
- keys_raw: bfloat16 [24576, 4096], P('dp', 'mp'), may hold values from -6 to 6
- values: bfloat16 [24576, 4096], P('dp', 'mp'), may hold values from -6 to 6
- grad_out: bfloat16 [24576, 6144], P('dp', 'mp'), may hold values from -16 to 16
- out_weight: bfloat16 [6144, 4096], P('dp', 'mp'), may hold values from -0.09375 to 0.09375
- norm_gains: float32 [2, 128], replicated, may hold values from 0.5 to 5
Outputs:
- queries_grad: bfloat16 [24576, 4096], P('dp', 'mp')
- keys_grad: bfloat16 [24576, 4096], P('dp', 'mp')
- values_grad: bfloat16 [24576, 4096], P('dp', 'mp')
- weight_grad: float32 [6144, 4096], P('dp', 'mp')
- gains_grad: float32 [2, 128], replicated
The draws below stay inside these ranges and needn't reach their ends.
All inputs are finite; a program needn't handle non-finite values.
Results may differ from the reference program's by a relative error of at most 0.034.
The reference program's roundings to bfloat16 on the way (of `prob_low`, `attn`, `grad_attn` and `score_grad`) count: a program that leaves them out, or rounds other values in their place, can miss the bound.
Values may be sent and summed in bfloat16 or wider, within the bound.
No kernel may reach another device: no remote copies, remote signals or barrier semaphores. Data moves between devices by JAX's collectives and lax.ppermute only.
A program may use at most 64 MiB of HBM per device.

```python
import math
import jax
import jax.numpy as jnp
from jax import lax

D = 6144
HEADS = 32
HD = 128
PATCH = 256
TOK_DEV = 768
TOKENS = 24576
N_DP = 32


def shared_base(key):
    return jax.random.normal(jax.random.fold_in(key, 17), (TOKENS, HEADS * HD), jnp.float32)


def draw_keys_raw(key, part):
    base = shared_base(key)
    return jnp.clip(base, -6.0, 6.0).astype(jnp.bfloat16)


def draw_queries_raw(key, part):
    key = jax.random.fold_in(key, 1)
    fresh = jax.random.normal(key, (TOKENS, HEADS * HD), jnp.float32)
    return jnp.clip(fresh, -6.0, 6.0).astype(jnp.bfloat16)


def draw_norm_gains(key, part):
    key = jax.random.fold_in(key, 3)
    return jnp.exp(jax.random.uniform(key, (2, HD), jnp.float32, math.log(0.6), math.log(1.6)))


def spiked(values, rng, source, target, parts, factor):
    owner, partner = [(jnp.arange(values.shape[axis_at]) // (values.shape[axis_at] // parts)).reshape([-1 if axis == axis_at else 1 for axis in range(values.ndim)]) for axis_at in (source, target)]
    chosen = jax.random.permutation(rng, parts)[partner]
    strong = (owner == chosen) | (owner == (partner + parts // 2) % parts)
    return jnp.where(strong, factor * values, values)


def steps_of(stream_key, extent, split, least, high):
    loudness, own = 1.0, jax.random.fold_in(stream_key, 6)
    for dim, parts in split:
        steps = jnp.exp(jax.random.uniform(jax.random.fold_in(own, dim), (parts,), jnp.float32, least / len(split), high / len(split)))
        loudness = loudness * jnp.repeat(steps, extent[dim] // parts).reshape([-1 if axis == dim else 1 for axis in range(len(extent))])
    return loudness


def centred(own_key, extent, spread, most, cuts=(), dtype=jnp.bfloat16):
    entries = jax.random.normal(own_key, extent, jnp.float32) * spread
    if len(cuts) > 0:
        entries = steps_of(own_key, extent, cuts, -0.22, 0.18) * entries
    return jnp.clip(entries, min=-most, max=most).astype(dtype)


def heavy_noise(stream_key, dims, scale, bound, cuts, heavy, held_as=jnp.bfloat16):
    entries = scale * jax.random.normal(stream_key, dims, jnp.float32)
    if cuts:
        entries = entries * steps_of(stream_key, dims, cuts, -0.22, 0.18)
    return jnp.clip(spiked(entries, jax.random.fold_in(stream_key, 3), *heavy), -bound, bound).astype(held_as)


def setup_inputs(seed: int = 0) -> dict:
    key_list = jax.random.split(jax.random.key(seed), 7)
    return {
        "queries_raw": draw_queries_raw(jax.random.fold_in(key_list[6], 71), 0),
        "keys_raw": draw_keys_raw(jax.random.fold_in(key_list[6], 71), 0),
        "values": centred(key_list[2], (TOKENS, HEADS * HD), 1.0, 6.0, ((0, 32), (1, 16))),
        "grad_out": heavy_noise(key_list[3], (TOKENS, D), 2.0, 16.0, ((0, 32), (1, 16)), (0, 1, 32, 2.75)),
        "out_weight": centred(key_list[4], (D, HEADS * HD), (HEADS * HD) ** -0.5, 0.09375, ((0, 32), (1, 16))),
        "norm_gains": draw_norm_gains(jax.random.fold_in(key_list[6], 71), 0),
    }


EPSILON = 1e-06

def normalize(raw, gain):
    values32 = raw.astype(jnp.float32)
    center = values32 - lax.optimization_barrier(jnp.mean(values32, axis=-1, keepdims=True))
    inverse = lax.rsqrt(lax.optimization_barrier(jnp.mean(center * center, axis=-1, keepdims=True)) + EPSILON)
    unit = center * inverse
    return (unit, inverse, (unit * gain).astype(jnp.bfloat16))

def unnormalize(grad, unit, inverse, gain):
    scaled = grad * gain
    centered = scaled - lax.optimization_barrier(jnp.mean(scaled, axis=-1, keepdims=True))
    return ((centered - unit * lax.optimization_barrier(jnp.mean(scaled * unit, axis=-1, keepdims=True))) * inverse).astype(jnp.bfloat16)

def heads_view(array):
    return array.reshape(array.shape[0] // PATCH, PATCH, array.shape[1] // HD, HD)

def attend(queries_raw, keys_raw, values, norm_gains):
    scale = HD ** (-0.5)
    q_unit, q_inverse, q_norm = normalize(heads_view(queries_raw), norm_gains[0])
    k_unit, k_inverse, k_norm = normalize(heads_view(keys_raw), norm_gains[1])
    value_view = heads_view(values)
    scores = jnp.einsum('iphd,iqhd->ihpq', q_norm.astype(jnp.float32), k_norm.astype(jnp.float32)) * scale
    peak = lax.optimization_barrier(jnp.max(scores, axis=-1, keepdims=True))
    expo = jnp.exp(scores - peak)
    prob = expo / lax.optimization_barrier(jnp.sum(expo, axis=-1, keepdims=True))
    prob_low = prob.astype(jnp.bfloat16)
    attn = jnp.einsum('ihpq,iqhd->iphd', prob_low.astype(jnp.float32), value_view.astype(jnp.float32)).astype(jnp.bfloat16)
    return (q_unit, q_inverse, q_norm, k_unit, k_inverse, k_norm, value_view, prob, prob_low, attn)

def backward(state, grad_attn, norm_gains):
    q_unit, q_inverse, q_norm, k_unit, k_inverse, k_norm, value_view, prob, prob_low, attn = state
    scale = HD ** (-0.5)
    tokens = grad_attn.shape[0]
    grad_view = heads_view(grad_attn)
    grad32 = grad_view.astype(jnp.float32)
    values_grad = jnp.einsum('ihpq,iphd->iqhd', prob_low.astype(jnp.float32), grad32).astype(jnp.bfloat16)
    product = jnp.einsum('iphd,iqhd->ihpq', grad32, value_view.astype(jnp.float32))
    delta = lax.optimization_barrier(jnp.sum(grad32 * attn.astype(jnp.float32), axis=-1))
    delta = jnp.transpose(delta, (0, 2, 1))[..., None]
    score_grad = (prob * (product - delta)).astype(jnp.bfloat16)
    score32 = score_grad.astype(jnp.float32)
    qn_grad = jnp.einsum('ihpq,iqhd->iphd', score32, k_norm.astype(jnp.float32)) * scale
    kn_grad = jnp.einsum('ihpq,iphd->iqhd', score32, q_norm.astype(jnp.float32)) * scale
    terms = jnp.stack([lax.optimization_barrier(jnp.sum(qn_grad * q_unit, axis=(0, 1, 2))), lax.optimization_barrier(jnp.sum(kn_grad * k_unit, axis=(0, 1, 2)))])
    queries_grad = unnormalize(qn_grad, q_unit, q_inverse, norm_gains[0]).reshape(tokens, -1)
    keys_grad = unnormalize(kn_grad, k_unit, k_inverse, norm_gains[1]).reshape(tokens, -1)
    return (queries_grad, keys_grad, values_grad.reshape(tokens, -1), terms)

def reference(queries_raw, keys_raw, values, grad_out, out_weight, norm_gains):
    width = HEADS * HD

    def group(carry, pieces):
        weight_sum, gain_sum = carry
        q_block, k_block, v_block, grad_block = pieces
        state = attend(q_block, k_block, v_block, norm_gains)
        attn_flat = state[-1].reshape(TOK_DEV, width)
        grad_attn = jnp.dot(grad_block, out_weight, preferred_element_type=jnp.float32).astype(jnp.bfloat16)
        partial_low = jnp.dot(grad_block.T, attn_flat, preferred_element_type=jnp.float32).astype(jnp.bfloat16)
        partial_low = lax.optimization_barrier(partial_low)
        q_grad, k_grad, v_grad, terms = backward(state, grad_attn, norm_gains)
        return ((weight_sum + partial_low.astype(jnp.float32), gain_sum + terms), (q_grad, k_grad, v_grad))
    start = (jnp.zeros((D, width), jnp.float32), jnp.zeros((2, HD), jnp.float32))
    pieces = (queries_raw.reshape(N_DP, TOK_DEV, width), keys_raw.reshape(N_DP, TOK_DEV, width), values.reshape(N_DP, TOK_DEV, width), grad_out.reshape(N_DP, TOK_DEV, D))
    (weight_grad, gains_grad), (q_all, k_all, v_all) = lax.scan(group, start, pieces)
    return (q_all.reshape(TOKENS, width), k_all.reshape(TOKENS, width), v_all.reshape(TOKENS, width), weight_grad, gains_grad)
```

```python
import jax
import jax.numpy as jnp
from jax import lax
from jax.experimental import pallas as pl
from jax.experimental.pallas import tpu as pltpu
from jax.sharding import Mesh, PartitionSpec as P

HD = 128
PATCH = 256
EPSILON = 1e-06
AXES = ("yl", "z", "yh", "x", "c")
SIZES = (2, 16, 2, 4, 2)


def normalize(raw, gain):
    values32 = raw.astype(jnp.float32)
    center = values32 - jnp.mean(values32, axis=-1, keepdims=True)
    inverse = lax.rsqrt(jnp.mean(center * center, axis=-1, keepdims=True) + EPSILON)
    unit = center * inverse
    return (unit, inverse, (unit * gain).astype(jnp.bfloat16))


def unnormalize(grad, unit, inverse, gain):
    scaled = grad * gain
    centered = scaled - jnp.mean(scaled, axis=-1, keepdims=True)
    return ((centered - unit * jnp.mean(scaled * unit, axis=-1, keepdims=True)) * inverse).astype(
        jnp.bfloat16
    )


def heads_view(array):
    return array.reshape(array.shape[0] // PATCH, PATCH, array.shape[1] // HD, HD)


def attend(queries_raw, keys_raw, values, norm_gains):
    scale = HD ** (-0.5)
    q_unit, q_inverse, q_norm = normalize(heads_view(queries_raw), norm_gains[0])
    k_unit, k_inverse, k_norm = normalize(heads_view(keys_raw), norm_gains[1])
    value_view = heads_view(values)
    scores = (
        jnp.einsum("iphd,iqhd->ihpq", q_norm, k_norm, preferred_element_type=jnp.float32) * scale
    )
    peak = jnp.max(scores, axis=-1, keepdims=True)
    expo = jnp.exp(scores - peak)
    prob = expo / jnp.sum(expo, axis=-1, keepdims=True)
    prob_low = prob.astype(jnp.bfloat16)
    attn = jnp.einsum(
        "ihpq,iqhd->iphd", prob_low, value_view, preferred_element_type=jnp.float32
    ).astype(jnp.bfloat16)
    return (q_unit, q_inverse, q_norm, k_unit, k_inverse, k_norm, value_view, prob, prob_low, attn)


def backward(state, grad_attn, norm_gains):
    q_unit, q_inverse, q_norm, k_unit, k_inverse, k_norm, value_view, prob, prob_low, attn = state
    scale = HD ** (-0.5)
    tokens = grad_attn.shape[0]
    grad_view = heads_view(grad_attn)
    values_grad = jnp.einsum(
        "ihpq,iphd->iqhd", prob_low, grad_view, preferred_element_type=jnp.float32
    ).astype(jnp.bfloat16)
    product = jnp.einsum(
        "iphd,iqhd->ihpq", grad_view, value_view, preferred_element_type=jnp.float32
    )
    delta = jnp.sum(grad_view.astype(jnp.float32) * attn.astype(jnp.float32), axis=-1)
    delta = jnp.transpose(delta, (0, 2, 1))[..., None]
    score_grad = (prob * (product - delta)).astype(jnp.bfloat16)
    qn_grad = (
        jnp.einsum("ihpq,iqhd->iphd", score_grad, k_norm, preferred_element_type=jnp.float32)
        * scale
    )
    kn_grad = (
        jnp.einsum("ihpq,iphd->iqhd", score_grad, q_norm, preferred_element_type=jnp.float32)
        * scale
    )
    terms = jnp.stack(
        [jnp.sum(qn_grad * q_unit, axis=(0, 1, 2)), jnp.sum(kn_grad * k_unit, axis=(0, 1, 2))]
    )
    queries_grad = unnormalize(qn_grad, q_unit, q_inverse, norm_gains[0]).reshape(tokens, -1)
    keys_grad = unnormalize(kn_grad, k_unit, k_inverse, norm_gains[1]).reshape(tokens, -1)
    return (queries_grad, keys_grad, values_grad.reshape(tokens, -1), terms)


def swap_y(array, target):
    pairs = []
    for low in range(2):
        for high in range(2):
            to_low, to_high = target(low, high)
            pairs.append((low * 2 + high, to_low * 2 + to_high))
    return lax.ppermute(array, ("yl", "yh"), pairs)


def transpose_y(array):
    return swap_y(array, lambda low, high: (high, low))


def sum_over(array, axis, count):
    spread = lax.all_to_all(jnp.broadcast_to(array[None], (count,) + array.shape), axis, 0, 0)
    return jnp.sum(spread, axis=0)


def product_kernel(grad_ref, weight_ref, attn_ref, part_ref, wgrad_ref, total):
    step = pl.program_id(0)

    @pl.when(step == 0)
    def _():
        total[...] = jnp.zeros_like(total)

    weights = weight_ref[...]
    flipped = None
    for token in range(2):
        block = grad_ref[token, 0]
        total[token] += jnp.dot(block, weights, preferred_element_type=jnp.float32)
        term = jnp.dot(attn_ref[token], block, preferred_element_type=jnp.float32)
        flipped = term if flipped is None else flipped + term
    wgrad_ref[...] = flipped.T.astype(wgrad_ref.dtype)

    @pl.when(step == pl.num_programs(0) - 1)
    def _():
        part_ref[...] = total[...].astype(part_ref.dtype)


def products(grads, weights, attn_flipped):
    _, blocks, tokens, width = grads.shape
    heads = weights.shape[1]
    return pl.pallas_call(
        product_kernel,
        grid=(blocks,),
        in_specs=[
            pl.BlockSpec((2, 1, tokens, width), lambda k: (0, k, 0, 0)),
            pl.BlockSpec((width, heads), lambda k: (k, 0)),
            pl.BlockSpec((2, heads, tokens), lambda k: (0, 0, 0)),
        ],
        out_specs=[
            pl.BlockSpec((2, tokens, heads), lambda k: (0, 0, 0)),
            pl.BlockSpec((width, heads), lambda k: (k, 0)),
        ],
        out_shape=[
            jax.ShapeDtypeStruct((2, tokens, heads), jnp.bfloat16),
            jax.ShapeDtypeStruct((blocks * width, heads), jnp.bfloat16),
        ],
        scratch_shapes=[pltpu.VMEM((2, tokens, heads), jnp.float32)],
        compiler_params=pltpu.CompilerParams(vmem_limit_bytes=32 * 1024 * 1024),
        cost_estimate=pl.CostEstimate(
            flops=8 * blocks * tokens * width * heads,
            bytes_accessed=2 * (2 * blocks * tokens * width + 2 * blocks * width * heads),
            transcendentals=0,
        ),
    )(grads, weights, attn_flipped)


def per_device(queries_raw, keys_raw, values, grad_out, out_weight, norm_gains):
    high = lax.axis_index("yh")
    full_grad = lax.all_gather(grad_out, ("yl", "x", "c"), axis=0)
    full_grad = full_grad.reshape((2, 8) + grad_out.shape)
    own_rows = transpose_y(out_weight)
    half = own_rows.shape[0] // 2
    first = lax.all_gather(own_rows[:half], "z", axis=0)
    second = lax.all_gather(own_rows[half:], "z", axis=0)
    weights = jnp.concatenate([first, second], axis=1).reshape(-1, own_rows.shape[1])

    state = attend(queries_raw, keys_raw, values, norm_gains)
    tokens = queries_raw.shape[0]
    attn_flat = state[-1].reshape(tokens, -1)
    attn_same = transpose_y(attn_flat)
    attn_other = swap_y(attn_flat, lambda low, up: (up, 1 - low))
    both = jnp.stack([attn_same.T, attn_other.T])
    both = jnp.where(high == 0, both, both[::-1])

    parts, wgrad = products(full_grad, weights, both)
    shard = lax.psum_scatter(wgrad, "z", scatter_dimension=0, tiled=True)

    parts = jnp.where(high == 0, parts, parts[::-1])
    came_same = transpose_y(parts[0])
    came_other = swap_y(parts[1], lambda low, up: (1 - up, low))
    grad_attn = (came_same.astype(jnp.float32) + came_other.astype(jnp.float32)).astype(
        jnp.bfloat16
    )
    queries_grad, keys_grad, values_grad, terms = backward(state, grad_attn, norm_gains)
    gains_grad = sum_over(sum_over(terms, "z", 16), ("yl", "yh", "x", "c"), 32)
    weight_grad = transpose_y(shard).astype(jnp.float32)
    return (queries_grad, keys_grad, values_grad, weight_grad, gains_grad)


def solution(mesh):
    fine = Mesh(mesh.devices.reshape(SIZES), AXES)
    spec = P(("yl", "z"), ("yh", "x", "c"))
    return jax.shard_map(
        per_device,
        mesh=fine,
        in_specs=(spec, spec, spec, spec, spec, P()),
        out_specs=(spec, spec, spec, spec, P()),
        check_vma=False,
    )
```

```python
import jax
import jax.numpy as jnp
from jax import lax
from jax.experimental import pallas as pl
from jax.experimental.pallas import tpu as pltpu
from jax.sharding import Mesh, PartitionSpec as P

HD = 128
PATCH = 256
EPSILON = 1e-06
SCALE = HD ** (-0.5)
AXES = ("yl", "z", "yh", "x", "c")
SIZES = (2, 16, 2, 4, 2)
VMEM_LIMIT = 56 * 1024 * 1024


def normalize(raw, gain):
    values32 = raw.astype(jnp.float32)
    center = values32 - jnp.mean(values32, axis=-1, keepdims=True)
    inverse = lax.rsqrt(jnp.mean(center * center, axis=-1, keepdims=True) + EPSILON)
    unit = center * inverse
    return (unit, inverse, (unit * gain).astype(jnp.bfloat16))


def unnormalize(grad, unit, inverse, gain):
    scaled = grad * gain
    centered = scaled - jnp.mean(scaled, axis=-1, keepdims=True)
    return (centered - unit * jnp.mean(scaled * unit, axis=-1, keepdims=True)) * inverse


def product(left, right, left_dim, right_dim):
    return lax.dot_general(
        left, right, (((left_dim,), (right_dim,)), ((), ())), preferred_element_type=jnp.float32
    )


def softmax(q_norm, k_norm):
    scores = product(q_norm, k_norm, 1, 1) * SCALE
    expo = jnp.exp(scores - jnp.max(scores, axis=-1, keepdims=True))
    return expo / jnp.sum(expo, axis=-1, keepdims=True)


def forward_kernel(q_ref, k_ref, v_ref, gains_ref, attn_ref):
    for head in range(q_ref.shape[1] // HD):
        cols = slice(head * HD, (head + 1) * HD)
        _, _, q_norm = normalize(q_ref[:, cols], gains_ref[0:1, :])
        _, _, k_norm = normalize(k_ref[:, cols], gains_ref[1:2, :])
        prob_low = softmax(q_norm, k_norm).astype(jnp.bfloat16)
        attn = product(prob_low, v_ref[:, cols], 1, 0)
        attn_ref[cols, :] = attn.T.astype(jnp.bfloat16)


def forward(queries_raw, keys_raw, values, norm_gains):
    tokens, width = queries_raw.shape
    block = pl.BlockSpec((PATCH, width), lambda i: (i, 0))
    return pl.pallas_call(
        forward_kernel,
        grid=(tokens // PATCH,),
        in_specs=[block, block, block, pl.BlockSpec((2, HD), lambda i: (0, 0))],
        out_specs=pl.BlockSpec((width, PATCH), lambda i: (0, i)),
        out_shape=jax.ShapeDtypeStruct((width, tokens), jnp.bfloat16),
        compiler_params=pltpu.CompilerParams(vmem_limit_bytes=VMEM_LIMIT),
    )(queries_raw, keys_raw, values, norm_gains)


def backward_kernel(
    q_ref, k_ref, v_ref, one_ref, two_ref, gains_ref, qg_ref, kg_ref, vg_ref, terms_ref
):
    @pl.when(pl.program_id(0) == 0)
    def _():
        terms_ref[...] = jnp.zeros_like(terms_ref)

    q_gain, k_gain = gains_ref[0:1, :], gains_ref[1:2, :]
    for head in range(q_ref.shape[1] // HD):
        cols = slice(head * HD, (head + 1) * HD)
        value = v_ref[:, cols]
        q_unit, q_inverse, q_norm = normalize(q_ref[:, cols], q_gain)
        k_unit, k_inverse, k_norm = normalize(k_ref[:, cols], k_gain)
        prob = softmax(q_norm, k_norm)
        prob_low = prob.astype(jnp.bfloat16)
        attn = product(prob_low, value, 1, 0).astype(jnp.bfloat16)
        grad = one_ref[:, cols].astype(jnp.float32) + two_ref[:, cols].astype(jnp.float32)
        grad = grad.astype(jnp.bfloat16)
        vg_ref[:, cols] = product(prob_low, grad, 0, 0).astype(jnp.bfloat16)
        delta = jnp.sum(
            grad.astype(jnp.float32) * attn.astype(jnp.float32), axis=-1, keepdims=True
        )
        score_grad = (prob * (product(grad, value, 1, 1) - delta)).astype(jnp.bfloat16)
        qn_grad = product(score_grad, k_norm, 1, 0) * SCALE
        kn_grad = product(score_grad, q_norm, 0, 0) * SCALE
        terms_ref[0:1, :] += jnp.sum(qn_grad * q_unit, axis=0, keepdims=True)
        terms_ref[1:2, :] += jnp.sum(kn_grad * k_unit, axis=0, keepdims=True)
        qg_ref[:, cols] = unnormalize(qn_grad, q_unit, q_inverse, q_gain).astype(jnp.bfloat16)
        kg_ref[:, cols] = unnormalize(kn_grad, k_unit, k_inverse, k_gain).astype(jnp.bfloat16)


def backward(queries_raw, keys_raw, values, part_one, part_two, norm_gains):
    tokens, width = queries_raw.shape
    block = pl.BlockSpec((PATCH, width), lambda i: (i, 0))
    gains = pl.BlockSpec((2, HD), lambda i: (0, 0))
    out = jax.ShapeDtypeStruct((tokens, width), jnp.bfloat16)
    return pl.pallas_call(
        backward_kernel,
        grid=(tokens // PATCH,),
        in_specs=[block] * 5 + [gains],
        out_specs=[block, block, block, gains],
        out_shape=[out, out, out, jax.ShapeDtypeStruct((2, HD), jnp.float32)],
        compiler_params=pltpu.CompilerParams(vmem_limit_bytes=VMEM_LIMIT),
    )(queries_raw, keys_raw, values, part_one, part_two, norm_gains)


def products_kernel(
    high_ref, grad_ref, weight_ref, same_ref, other_ref, part_same_ref, part_other_ref,
    wgrad_ref, total_same, total_other,
):
    step = pl.program_id(0)

    @pl.when(step == 0)
    def _():
        total_same[...] = jnp.zeros_like(total_same)
        total_other[...] = jnp.zeros_like(total_other)

    high = high_ref[0]
    weights = weight_ref[...].reshape(grad_ref.shape[3], weight_ref.shape[3])
    block = grad_ref[high, 0]
    flipped = product(same_ref[...], block, 1, 0)
    total_same[...] += product(block, weights, 1, 0)
    block = grad_ref[1 - high, 0]
    flipped += product(other_ref[...], block, 1, 0)
    total_other[...] += product(block, weights, 1, 0)
    wgrad_ref[...] = flipped.T.astype(wgrad_ref.dtype).reshape(wgrad_ref.shape)

    @pl.when(step == pl.num_programs(0) - 1)
    def _():
        part_same_ref[...] = total_same[...].astype(part_same_ref.dtype)
        part_other_ref[...] = total_other[...].astype(part_other_ref.dtype)


def products(high, grads, weights, attn_same, attn_other):
    _, blocks, tokens, width = grads.shape
    rows, heads = weights.shape[2:]
    pair = pl.BlockSpec((2, 1, rows, heads), lambda k, high: (k % 2, k // 2, 0, 0))
    attn = pl.BlockSpec((heads, tokens), lambda k, high: (0, 0))
    part = pl.BlockSpec((tokens, heads), lambda k, high: (0, 0))
    return pl.pallas_call(
        products_kernel,
        grid_spec=pltpu.PrefetchScalarGridSpec(
            num_scalar_prefetch=1,
            grid=(blocks,),
            in_specs=[
                pl.BlockSpec((2, 1, tokens, width), lambda k, high: (0, k, 0, 0)),
                pair,
                attn,
                attn,
            ],
            out_specs=[part, part, pair],
            scratch_shapes=[pltpu.VMEM((tokens, heads), jnp.float32)] * 2,
        ),
        out_shape=[
            jax.ShapeDtypeStruct((tokens, heads), jnp.bfloat16),
            jax.ShapeDtypeStruct((tokens, heads), jnp.bfloat16),
            jax.ShapeDtypeStruct(weights.shape, jnp.bfloat16),
        ],
        compiler_params=pltpu.CompilerParams(vmem_limit_bytes=VMEM_LIMIT),
        cost_estimate=pl.CostEstimate(
            flops=8 * blocks * tokens * width * heads,
            bytes_accessed=2 * (2 * blocks * tokens * width + 2 * blocks * width * heads),
            transcendentals=0,
        ),
    )(high, grads, weights, attn_same, attn_other)


def permute(array, target):
    pairs = []
    for low in range(2):
        for z in range(16):
            for high in range(2):
                to_low, to_z, to_high = target(low, z, high)
                pairs.append(((low * 16 + z) * 2 + high, (to_low * 16 + to_z % 16) * 2 + to_high))
    return lax.ppermute(array, ("yl", "z", "yh"), pairs)


def along(array, step):
    return permute(array, lambda low, z, high: (low, z + step, high))


def turned(array, step):
    return permute(array, lambda low, z, high: (high, z + step, low))


def pick(array, index):
    return lax.dynamic_index_in_dim(array, index, 0, keepdims=False)


def rolled(blocks, shift):
    return lax.dynamic_slice_in_dim(
        jnp.stack(blocks + blocks), (4 - shift) % 4, 4, axis=0
    )


def gather_rows(out_weight, z):
    column = rolled([turned(out_weight, -4 * step) for step in range(4)], z // 4)
    before = along(column, 1)
    after = along(column, -1)
    far = jnp.concatenate([along(column[:2], 2), along(column[2:], -2)])
    return rolled([column, after, far, before], z % 4)


def scatter_rows(wgrad, z):
    own = pick(wgrad, z % 4)
    before = along(pick(wgrad, (z + 1) % 4), 1)
    after = along(pick(wgrad, (z + 3) % 4), -1)
    far = pick(wgrad, (z + 2) % 4)
    far = jnp.concatenate([along(far[:2], 2), along(far[2:], -2)])
    column = sum(term.astype(jnp.float32) for term in (own, before, after, far))
    column = column.astype(jnp.bfloat16)
    terms = [turned(pick(column, (z // 4 + step) % 4), 4 * step) for step in range(4)]
    return sum(term.astype(jnp.float32) for term in terms)


def sum_over(array, axis, count):
    spread = lax.all_to_all(jnp.broadcast_to(array[None], (count,) + array.shape), axis, 0, 0)
    return jnp.sum(spread, axis=0)


def per_device(queries_raw, keys_raw, values, grad_out, out_weight, norm_gains):
    z = lax.axis_index("z")
    high = lax.axis_index("yh").reshape(1)
    grads = lax.all_gather(grad_out, ("yl", "x", "c"), axis=0)
    grads = grads.reshape((2, 8) + grad_out.shape)
    weights = gather_rows(out_weight, z)

    attn = forward(queries_raw, keys_raw, values, norm_gains)
    attn_same = turned(attn, 0)
    attn_other = permute(attn, lambda low, z, up: (up, z, 1 - low))

    part_same, part_other, wgrad = products(high, grads, weights, attn_same, attn_other)
    came_same = turned(part_same, 0)
    came_other = permute(part_other, lambda low, z, up: (1 - up, z, low))
    weight_grad = scatter_rows(wgrad, z)
    queries_grad, keys_grad, values_grad, terms = backward(
        queries_raw, keys_raw, values, came_same, came_other, norm_gains
    )
    gains_grad = sum_over(sum_over(terms, "z", 16), ("yl", "yh", "x", "c"), 32)
    return (queries_grad, keys_grad, values_grad, weight_grad, gains_grad)


def solution(mesh):
    fine = Mesh(mesh.devices.reshape(SIZES), AXES)
    spec = P(("yl", "z"), ("yh", "x", "c"))
    return jax.shard_map(
        per_device,
        mesh=fine,
        in_specs=(spec, spec, spec, spec, spec, P()),
        out_specs=(spec, spec, spec, spec, P()),
        check_vma=False,
    )
```

```python
import jax
import jax.numpy as jnp
from jax import lax
from jax.experimental import pallas as pl
from jax.experimental.pallas import tpu as pltpu
from jax.sharding import Mesh, PartitionSpec as P

HD = 128
PATCH = 256
EPSILON = 1e-06
SCALE = HD ** (-0.5)
AXES = ("yl", "za", "zb", "yh", "x", "c")
SIZES = (2, 8, 2, 2, 4, 2)
VMEM_LIMIT = 56 * 1024 * 1024


def normalize(raw, gain):
    values32 = raw.astype(jnp.float32)
    center = values32 - jnp.mean(values32, axis=-1, keepdims=True)
    inverse = lax.rsqrt(jnp.mean(center * center, axis=-1, keepdims=True) + EPSILON)
    unit = center * inverse
    return (unit, inverse, (unit * gain).astype(jnp.bfloat16))


def unnormalize(grad, unit, inverse, gain):
    scaled = grad * gain
    centered = scaled - jnp.mean(scaled, axis=-1, keepdims=True)
    return (centered - unit * jnp.mean(scaled * unit, axis=-1, keepdims=True)) * inverse


def product(left, right, left_dim, right_dim):
    return lax.dot_general(
        left, right, (((left_dim,), (right_dim,)), ((), ())), preferred_element_type=jnp.float32
    )


def softmax(q_norm, k_norm):
    scores = product(q_norm, k_norm, 1, 1) * SCALE
    expo = jnp.exp(scores - jnp.max(scores, axis=-1, keepdims=True))
    return expo / jnp.sum(expo, axis=-1, keepdims=True)


def forward_kernel(q_ref, k_ref, v_ref, gains_ref, attn_ref):
    for head in range(q_ref.shape[1] // HD):
        cols = slice(head * HD, (head + 1) * HD)
        _, _, q_norm = normalize(q_ref[:, cols], gains_ref[0:1, :])
        _, _, k_norm = normalize(k_ref[:, cols], gains_ref[1:2, :])
        prob_low = softmax(q_norm, k_norm).astype(jnp.bfloat16)
        attn_ref[:, cols] = product(prob_low, v_ref[:, cols], 1, 0).astype(jnp.bfloat16)


def forward(queries_raw, keys_raw, values, norm_gains):
    tokens, width = queries_raw.shape
    block = pl.BlockSpec((PATCH, width), lambda i: (i, 0))
    return pl.pallas_call(
        forward_kernel,
        grid=(tokens // PATCH,),
        in_specs=[block, block, block, pl.BlockSpec((2, HD), lambda i: (0, 0))],
        out_specs=block,
        out_shape=jax.ShapeDtypeStruct((tokens, width), jnp.bfloat16),
        compiler_params=pltpu.CompilerParams(vmem_limit_bytes=VMEM_LIMIT),
    )(queries_raw, keys_raw, values, norm_gains)


def backward_kernel(
    q_ref, k_ref, v_ref, p0_ref, p1_ref, p2_ref, p3_ref, gains_ref,
    qg_ref, kg_ref, vg_ref, terms_ref,
):
    @pl.when(pl.program_id(0) == 0)
    def _():
        terms_ref[...] = jnp.zeros_like(terms_ref)

    q_gain, k_gain = gains_ref[0:1, :], gains_ref[1:2, :]
    for head in range(q_ref.shape[1] // HD):
        cols = slice(head * HD, (head + 1) * HD)
        value = v_ref[:, cols]
        q_unit, q_inverse, q_norm = normalize(q_ref[:, cols], q_gain)
        k_unit, k_inverse, k_norm = normalize(k_ref[:, cols], k_gain)
        prob = softmax(q_norm, k_norm)
        prob_low = prob.astype(jnp.bfloat16)
        attn = product(prob_low, value, 1, 0).astype(jnp.bfloat16)
        grad = sum(ref[cols, :].astype(jnp.float32) for ref in (p0_ref, p1_ref, p2_ref, p3_ref))
        grad = grad.T.astype(jnp.bfloat16)
        vg_ref[:, cols] = product(prob_low, grad, 0, 0).astype(jnp.bfloat16)
        delta = jnp.sum(
            grad.astype(jnp.float32) * attn.astype(jnp.float32), axis=-1, keepdims=True
        )
        score_grad = (prob * (product(grad, value, 1, 1) - delta)).astype(jnp.bfloat16)
        qn_grad = product(score_grad, k_norm, 1, 0) * SCALE
        kn_grad = product(score_grad, q_norm, 0, 0) * SCALE
        terms_ref[0:1, :] += jnp.sum(qn_grad * q_unit, axis=0, keepdims=True)
        terms_ref[1:2, :] += jnp.sum(kn_grad * k_unit, axis=0, keepdims=True)
        qg_ref[:, cols] = unnormalize(qn_grad, q_unit, q_inverse, q_gain).astype(jnp.bfloat16)
        kg_ref[:, cols] = unnormalize(kn_grad, k_unit, k_inverse, k_gain).astype(jnp.bfloat16)


def backward(queries_raw, keys_raw, values, parts, norm_gains):
    tokens, width = queries_raw.shape
    block = pl.BlockSpec((PATCH, width), lambda i: (i, 0))
    part = pl.BlockSpec((width, PATCH), lambda i: (0, i))
    gains = pl.BlockSpec((2, HD), lambda i: (0, 0))
    out = jax.ShapeDtypeStruct((tokens, width), jnp.bfloat16)
    return pl.pallas_call(
        backward_kernel,
        grid=(tokens // PATCH,),
        in_specs=[block] * 3 + [part] * 4 + [gains],
        out_specs=[block, block, block, gains],
        out_shape=[out, out, out, jax.ShapeDtypeStruct((2, HD), jnp.float32)],
        compiler_params=pltpu.CompilerParams(vmem_limit_bytes=VMEM_LIMIT),
    )(queries_raw, keys_raw, values, *parts, norm_gains)


def flip_kernel(parity_ref, grad_ref, keep_ref, give_ref, flipped):
    rows = keep_ref.shape[0]
    for half in range(2):
        block = grad_ref[...].T[half * rows : (half + 1) * rows]
        flipped[half] = block
    keep_ref[...] = flipped[parity_ref[0]]
    give_ref[...] = flipped[1 - parity_ref[0]]


def flip(parity, grad_out):
    tokens, width = grad_out.shape
    half = jax.ShapeDtypeStruct((width // 2, tokens), grad_out.dtype)
    return pl.pallas_call(
        flip_kernel,
        in_specs=[pl.BlockSpec(memory_space=pltpu.SMEM), pl.BlockSpec(memory_space=pltpu.VMEM)],
        out_specs=[pl.BlockSpec(memory_space=pltpu.VMEM)] * 2,
        out_shape=[half, half],
        scratch_shapes=[pltpu.VMEM((2, width // 2, tokens), grad_out.dtype)],
        compiler_params=pltpu.CompilerParams(vmem_limit_bytes=VMEM_LIMIT),
    )(parity, grad_out)


def products_kernel(
    high_ref, grad_ref, weight_ref, same_ref, other_ref, ps0_ref, ps1_ref, po0_ref, po1_ref,
    wgrad_ref, total,
):
    step = pl.program_id(0)

    @pl.when(step == 0)
    def _():
        total[...] = jnp.zeros_like(total)

    high = high_ref[0]
    weights = weight_ref[0].T
    wgrad = None
    for index, (low, attn_ref) in enumerate(((high, same_ref), (1 - high, other_ref))):
        for z in range(2):
            block = grad_ref[low, 0, z]
            term = product(block, attn_ref[z], 1, 0)
            wgrad = term if wgrad is None else wgrad + term
            total[index * 2 + z] += product(weights, block, 1, 0)
    wgrad_ref[0] = wgrad.astype(wgrad_ref.dtype)

    @pl.when(step == pl.num_programs(0) - 1)
    def _():
        for index, ref in enumerate((ps0_ref, ps1_ref, po0_ref, po1_ref)):
            ref[...] = total[index].astype(ref.dtype)


def products(high, grads, weights, attn_same, attn_other):
    _, blocks, _, rows, tokens = grads.shape
    heads = weights.shape[2]
    slab = pl.BlockSpec((1, rows, heads), lambda k, high: (k, 0, 0))
    attn = pl.BlockSpec((2, tokens, heads), lambda k, high: (0, 0, 0))
    part = pl.BlockSpec((heads, tokens), lambda k, high: (0, 0))
    return pl.pallas_call(
        products_kernel,
        grid_spec=pltpu.PrefetchScalarGridSpec(
            num_scalar_prefetch=1,
            grid=(blocks,),
            in_specs=[
                pl.BlockSpec((2, 1, 2, rows, tokens), lambda k, high: (0, k, 0, 0, 0)),
                slab,
                attn,
                attn,
            ],
            out_specs=[part] * 4 + [slab],
            scratch_shapes=[pltpu.VMEM((4, heads, tokens), jnp.float32)],
        ),
        out_shape=[jax.ShapeDtypeStruct((heads, tokens), jnp.bfloat16)] * 4
        + [jax.ShapeDtypeStruct(weights.shape, jnp.bfloat16)],
        compiler_params=pltpu.CompilerParams(vmem_limit_bytes=VMEM_LIMIT),
        cost_estimate=pl.CostEstimate(
            flops=16 * blocks * tokens * rows * heads,
            bytes_accessed=2 * (4 * blocks * tokens * rows + 2 * blocks * rows * heads),
            transcendentals=0,
        ),
    )(high, grads, weights, attn_same, attn_other)


def permute(array, target):
    pairs = []
    for low in range(2):
        for z in range(2):
            for high in range(2):
                to_low, to_z, to_high = target(low, z, high)
                pairs.append(((low * 2 + z) * 2 + high, (to_low * 2 + to_z) * 2 + to_high))
    return lax.ppermute(array, ("yl", "zb", "yh"), pairs)


def turned(array):
    return permute(array, lambda low, z, high: (high, z, low))


def beside(array):
    return permute(array, lambda low, z, high: (low, 1 - z, high))


def sum_over(array, axis, count):
    spread = lax.all_to_all(jnp.broadcast_to(array[None], (count,) + array.shape), axis, 0, 0)
    return jnp.sum(spread, axis=0)


def per_device(queries_raw, keys_raw, values, grad_out, out_weight, norm_gains):
    high = lax.axis_index("yh").reshape(1)
    parity = lax.axis_index("zb").reshape(1)
    keep, give = flip(parity, grad_out)
    mine = jnp.stack([keep, beside(give)])
    grads = lax.all_gather(mine, ("yl", "x", "c"), axis=0)
    grads = grads.reshape((2, 8) + mine.shape)
    own_rows, _ = lax.optimization_barrier((turned(out_weight), mine))
    weights = lax.all_gather(own_rows, "za", axis=0)

    attn = forward(queries_raw, keys_raw, values, norm_gains)
    attn = jnp.stack([attn, beside(attn)])
    attn_same = turned(attn)
    attn_other = permute(attn, lambda low, z, up: (up, z, 1 - low))

    ps0, ps1, po0, po1, wgrad = products(high, grads, weights, attn_same, attn_other)
    shard = lax.psum_scatter(wgrad, "za", scatter_dimension=0)
    parts = [
        turned(ps0),
        permute(ps1, lambda low, z, up: (up, 1 - z, low)),
        permute(po0, lambda low, z, up: (1 - up, z, low)),
        permute(po1, lambda low, z, up: (1 - up, 1 - z, low)),
    ]
    queries_grad, keys_grad, values_grad, terms = backward(
        queries_raw, keys_raw, values, parts, norm_gains
    )
    gains_grad = sum_over(sum_over(terms, ("yl", "yh", "x", "c"), 32), ("za", "zb"), 16)
    weight_grad = turned(shard).astype(jnp.float32)
    return (queries_grad, keys_grad, values_grad, weight_grad, gains_grad)


def solution(mesh):
    fine = Mesh(mesh.devices.reshape(SIZES), AXES)
    spec = P(("yl", "za", "zb"), ("yh", "x", "c"))
    return jax.shard_map(
        per_device,
        mesh=fine,
        in_specs=(spec, spec, spec, spec, spec, P()),
        out_specs=(spec, spec, spec, spec, P()),
        check_vma=False,
    )
```

```python
import jax
import jax.numpy as jnp
from jax import lax
from jax.experimental import pallas as pl
from jax.experimental.pallas import tpu as pltpu
from jax.sharding import Mesh, PartitionSpec as P

HD = 128
PATCH = 256
EPSILON = 1e-06
SCALE = HD ** (-0.5)
AXES = ("yl", "za", "zb", "yh", "x", "c")
SIZES = (2, 4, 4, 2, 4, 2)
Z = ("za", "zb")
VMEM_LIMIT = 56 * 1024 * 1024


def normalize(raw, gain):
    values32 = raw.astype(jnp.float32)
    center = values32 - jnp.mean(values32, axis=-1, keepdims=True)
    inverse = lax.rsqrt(jnp.mean(center * center, axis=-1, keepdims=True) + EPSILON)
    unit = center * inverse
    return (unit, inverse, (unit * gain).astype(jnp.bfloat16))


def unnormalize(grad, unit, inverse, gain):
    scaled = grad * gain
    centered = scaled - jnp.mean(scaled, axis=-1, keepdims=True)
    return (centered - unit * jnp.mean(scaled * unit, axis=-1, keepdims=True)) * inverse


def product(left, right, left_dim, right_dim):
    return lax.dot_general(
        left, right, (((left_dim,), (right_dim,)), ((), ())), preferred_element_type=jnp.float32
    )


def softmax(q_norm, k_norm):
    scores = product(q_norm, k_norm, 1, 1) * SCALE
    expo = jnp.exp(scores - jnp.max(scores, axis=-1, keepdims=True))
    return expo / jnp.sum(expo, axis=-1, keepdims=True)


def forward_kernel(q_ref, k_ref, v_ref, gains_ref, attn_ref):
    for head in range(q_ref.shape[1] // HD):
        cols = slice(head * HD, (head + 1) * HD)
        _, _, q_norm = normalize(q_ref[:, cols], gains_ref[0:1, :])
        _, _, k_norm = normalize(k_ref[:, cols], gains_ref[1:2, :])
        prob_low = softmax(q_norm, k_norm).astype(jnp.bfloat16)
        attn = product(prob_low, v_ref[:, cols], 1, 0)
        attn_ref[cols, :] = attn.T.astype(jnp.bfloat16)


def forward(queries_raw, keys_raw, values, norm_gains):
    tokens, width = queries_raw.shape
    block = pl.BlockSpec((PATCH, width), lambda i: (i, 0))
    return pl.pallas_call(
        forward_kernel,
        grid=(tokens // PATCH,),
        in_specs=[block, block, block, pl.BlockSpec((2, HD), lambda i: (0, 0))],
        out_specs=pl.BlockSpec((width, PATCH), lambda i: (0, i)),
        out_shape=jax.ShapeDtypeStruct((width, tokens), jnp.bfloat16),
        compiler_params=pltpu.CompilerParams(vmem_limit_bytes=VMEM_LIMIT),
    )(queries_raw, keys_raw, values, norm_gains)


def backward_kernel(
    q_ref, k_ref, v_ref, one_ref, two_ref, gains_ref, qg_ref, kg_ref, vg_ref, terms_ref
):
    @pl.when(pl.program_id(0) == 0)
    def _():
        terms_ref[...] = jnp.zeros_like(terms_ref)

    q_gain, k_gain = gains_ref[0:1, :], gains_ref[1:2, :]
    for head in range(q_ref.shape[1] // HD):
        cols = slice(head * HD, (head + 1) * HD)
        value = v_ref[:, cols]
        q_unit, q_inverse, q_norm = normalize(q_ref[:, cols], q_gain)
        k_unit, k_inverse, k_norm = normalize(k_ref[:, cols], k_gain)
        prob = softmax(q_norm, k_norm)
        prob_low = prob.astype(jnp.bfloat16)
        attn = product(prob_low, value, 1, 0).astype(jnp.bfloat16)
        grad = one_ref[:, cols].astype(jnp.float32) + two_ref[:, cols].astype(jnp.float32)
        grad = grad.astype(jnp.bfloat16)
        vg_ref[:, cols] = product(prob_low, grad, 0, 0).astype(jnp.bfloat16)
        delta = jnp.sum(
            grad.astype(jnp.float32) * attn.astype(jnp.float32), axis=-1, keepdims=True
        )
        score_grad = (prob * (product(grad, value, 1, 1) - delta)).astype(jnp.bfloat16)
        qn_grad = product(score_grad, k_norm, 1, 0) * SCALE
        kn_grad = product(score_grad, q_norm, 0, 0) * SCALE
        terms_ref[0:1, :] += jnp.sum(qn_grad * q_unit, axis=0, keepdims=True)
        terms_ref[1:2, :] += jnp.sum(kn_grad * k_unit, axis=0, keepdims=True)
        qg_ref[:, cols] = unnormalize(qn_grad, q_unit, q_inverse, q_gain).astype(jnp.bfloat16)
        kg_ref[:, cols] = unnormalize(kn_grad, k_unit, k_inverse, k_gain).astype(jnp.bfloat16)


def backward(queries_raw, keys_raw, values, part_one, part_two, norm_gains):
    tokens, width = queries_raw.shape
    block = pl.BlockSpec((PATCH, width), lambda i: (i, 0))
    gains = pl.BlockSpec((2, HD), lambda i: (0, 0))
    out = jax.ShapeDtypeStruct((tokens, width), jnp.bfloat16)
    return pl.pallas_call(
        backward_kernel,
        grid=(tokens // PATCH,),
        in_specs=[block] * 5 + [gains],
        out_specs=[block, block, block, gains],
        out_shape=[out, out, out, jax.ShapeDtypeStruct((2, HD), jnp.float32)],
        compiler_params=pltpu.CompilerParams(vmem_limit_bytes=VMEM_LIMIT),
    )(queries_raw, keys_raw, values, part_one, part_two, norm_gains)


def weight_kernel(high_ref, grad_ref, same_ref, other_ref, wgrad_ref):
    high = high_ref[0]
    width = grad_ref.shape[4]
    for core in range(2):
        flipped = product(same_ref[...], grad_ref[high, 0, core], 1, 0)
        flipped += product(other_ref[...], grad_ref[1 - high, 0, core], 1, 0)
        wgrad_ref[core * width : (core + 1) * width] = flipped.T.astype(wgrad_ref.dtype)


def grad_block(grads):
    return pl.BlockSpec((2, 1) + grads.shape[2:], lambda x, high: (0, x, 0, 0, 0))


def weight_product(high, grads, attn_same, attn_other):
    _, blocks, cores, tokens, width = grads.shape
    heads = attn_same.shape[0]
    attn = pl.BlockSpec((heads, tokens), lambda x, high: (0, 0))
    return pl.pallas_call(
        weight_kernel,
        grid_spec=pltpu.PrefetchScalarGridSpec(
            num_scalar_prefetch=1,
            grid=(blocks,),
            in_specs=[grad_block(grads), attn, attn],
            out_specs=pl.BlockSpec((cores * width, heads), lambda x, high: (x, 0)),
        ),
        out_shape=jax.ShapeDtypeStruct((blocks * cores * width, heads), jnp.bfloat16),
        compiler_params=pltpu.CompilerParams(vmem_limit_bytes=VMEM_LIMIT),
        cost_estimate=pl.CostEstimate(
            flops=2 * grads.size * heads,
            bytes_accessed=2 * (grads.size + blocks * cores * width * heads),
            transcendentals=0,
        ),
    )(high, grads, attn_same, attn_other)


def token_kernel(high_ref, grad_ref, weight_ref, same_ref, other_ref, total):
    step = pl.program_id(0)
    high = high_ref[0]
    weights = weight_ref[...].reshape(-1, weight_ref.shape[3])
    for index, low in enumerate((high, 1 - high)):
        block = jnp.concatenate([grad_ref[low, 0, 0], grad_ref[low, 0, 1]], axis=1)
        term = product(block, weights, 1, 0)

        @pl.when(step == 0)
        def _():
            total[index] = term

        @pl.when(step > 0)
        def _():
            total[index] += term

    @pl.when(step == pl.num_programs(0) - 1)
    def _():
        same_ref[...] = total[0].astype(same_ref.dtype)
        other_ref[...] = total[1].astype(other_ref.dtype)


def token_product(high, grads, weights):
    _, blocks, _, tokens, _ = grads.shape
    fours, _, rows, heads = weights.shape
    out = jax.ShapeDtypeStruct((tokens, heads), jnp.bfloat16)
    return pl.pallas_call(
        token_kernel,
        grid_spec=pltpu.PrefetchScalarGridSpec(
            num_scalar_prefetch=1,
            grid=(blocks,),
            in_specs=[
                grad_block(grads),
                pl.BlockSpec((fours, 1, rows, heads), lambda x, high: (0, x, 0, 0)),
            ],
            out_specs=[pl.BlockSpec((tokens, heads), lambda x, high: (0, 0))] * 2,
            scratch_shapes=[pltpu.VMEM((2, tokens, heads), jnp.float32)],
        ),
        out_shape=[out, out],
        compiler_params=pltpu.CompilerParams(vmem_limit_bytes=VMEM_LIMIT),
        cost_estimate=pl.CostEstimate(
            flops=2 * grads.size * heads,
            bytes_accessed=2 * (grads.size + weights.size),
            transcendentals=0,
        ),
    )(high, grads, weights)


def swap_y(array, target):
    pairs = []
    for low in range(2):
        for high in range(2):
            to_low, to_high = target(low, high)
            pairs.append((low * 2 + high, to_low * 2 + to_high))
    return lax.ppermute(array, ("yl", "yh"), pairs)


def turned(array):
    return swap_y(array, lambda low, high: (high, low))


def along(array, step):
    return lax.ppermute(array, Z, [(z, (z + step) % 16) for z in range(16)])


def gather_rows(own_rows):
    column = lax.all_gather(own_rows, "za", axis=0)
    before = along(column, 1)
    after = along(column, -1)
    far = jnp.concatenate([along(column[:2], 2), along(column[2:], -2)])
    blocks = [column, after, far, before]
    shift = (4 - lax.axis_index("zb")) % 4
    return lax.dynamic_slice_in_dim(jnp.stack(blocks + blocks), shift, 4, axis=0)


def sum_over(array, axis, count):
    spread = lax.all_to_all(jnp.broadcast_to(array[None], (count,) + array.shape), axis, 0, 0)
    return jnp.sum(spread, axis=0)


def per_device(queries_raw, keys_raw, values, grad_out, out_weight, norm_gains):
    high = lax.axis_index("yh").reshape(1)
    grads = lax.all_gather(grad_out, ("yl", "x", "c"), axis=0)
    grads = grads.reshape((2, 4, 2) + grad_out.shape)

    attn = forward(queries_raw, keys_raw, values, norm_gains)
    attn_same = turned(attn)
    attn_other = swap_y(attn, lambda low, up: (up, 1 - low))
    weights = gather_rows(turned(out_weight))

    wgrad = weight_product(high, grads, attn_same, attn_other)
    shard = lax.psum_scatter(wgrad, Z, scatter_dimension=0, tiled=True)

    weights, _ = lax.optimization_barrier((weights, wgrad))
    part_same, part_other = token_product(high, grads, weights)
    came_same = turned(part_same)
    came_other = swap_y(part_other, lambda low, up: (1 - up, low))
    queries_grad, keys_grad, values_grad, terms = backward(
        queries_raw, keys_raw, values, came_same, came_other, norm_gains
    )
    gains_grad = sum_over(sum_over(terms, ("yl", "yh", "x", "c"), 32), Z, 16)
    shard, gains_grad = lax.optimization_barrier((shard, gains_grad))
    weight_grad = turned(shard).astype(jnp.float32)
    return (queries_grad, keys_grad, values_grad, weight_grad, gains_grad)


def solution(mesh):
    fine = Mesh(mesh.devices.reshape(SIZES), AXES)
    spec = P(("yl", "za", "zb"), ("yh", "x", "c"))
    return jax.shard_map(
        per_device,
        mesh=fine,
        in_specs=(spec, spec, spec, spec, spec, P()),
        out_specs=(spec, spec, spec, spec, P()),
        check_vma=False,
    )
```

```python
import jax
import jax.numpy as jnp
from jax import lax
from jax.experimental import pallas as pl
from jax.experimental.pallas import tpu as pltpu
from jax.sharding import Mesh, PartitionSpec as P

HD = 128
PATCH = 256
EPSILON = 1e-06
SCALE = HD ** (-0.5)
AXES = ("yl", "za", "zb", "yh", "x", "c")
SIZES = (2, 4, 4, 2, 4, 2)
Z = ("za", "zb")
VMEM_LIMIT = 56 * 1024 * 1024


def normalize(raw, gain):
    values32 = raw.astype(jnp.float32)
    center = values32 - jnp.mean(values32, axis=-1, keepdims=True)
    inverse = lax.rsqrt(jnp.mean(center * center, axis=-1, keepdims=True) + EPSILON)
    unit = center * inverse
    return (unit, inverse, (unit * gain).astype(jnp.bfloat16))


def unnormalize(grad, unit, inverse, gain):
    scaled = grad * gain
    centered = scaled - jnp.mean(scaled, axis=-1, keepdims=True)
    return (centered - unit * jnp.mean(scaled * unit, axis=-1, keepdims=True)) * inverse


def product(left, right, left_dim, right_dim):
    return lax.dot_general(
        left, right, (((left_dim,), (right_dim,)), ((), ())), preferred_element_type=jnp.float32
    )


def softmax(q_norm, k_norm):
    scores = product(q_norm, k_norm, 1, 1) * SCALE
    expo = jnp.exp(scores - jnp.max(scores, axis=-1, keepdims=True))
    return expo / jnp.sum(expo, axis=-1, keepdims=True)


def forward_kernel(q_ref, k_ref, v_ref, gains_ref, attn_ref):
    for head in range(q_ref.shape[1] // HD):
        cols = slice(head * HD, (head + 1) * HD)
        _, _, q_norm = normalize(q_ref[:, cols], gains_ref[0:1, :])
        _, _, k_norm = normalize(k_ref[:, cols], gains_ref[1:2, :])
        prob_low = softmax(q_norm, k_norm).astype(jnp.bfloat16)
        attn_ref[:, cols] = product(prob_low, v_ref[:, cols], 1, 0).astype(jnp.bfloat16)


def forward(queries_raw, keys_raw, values, norm_gains):
    tokens, width = queries_raw.shape
    block = pl.BlockSpec((PATCH, width), lambda i: (i, 0))
    return pl.pallas_call(
        forward_kernel,
        grid=(tokens // PATCH,),
        in_specs=[block, block, block, pl.BlockSpec((2, HD), lambda i: (0, 0))],
        out_specs=block,
        out_shape=jax.ShapeDtypeStruct((tokens, width), jnp.bfloat16),
        compiler_params=pltpu.CompilerParams(vmem_limit_bytes=VMEM_LIMIT),
    )(queries_raw, keys_raw, values, norm_gains)


def backward_kernel(
    q_ref, k_ref, v_ref, one_ref, two_ref, gains_ref, qg_ref, kg_ref, vg_ref, terms_ref
):
    @pl.when(pl.program_id(0) == 0)
    def _():
        terms_ref[...] = jnp.zeros_like(terms_ref)

    q_gain, k_gain = gains_ref[0:1, :], gains_ref[1:2, :]
    for head in range(q_ref.shape[1] // HD):
        cols = slice(head * HD, (head + 1) * HD)
        value = v_ref[:, cols]
        q_unit, q_inverse, q_norm = normalize(q_ref[:, cols], q_gain)
        k_unit, k_inverse, k_norm = normalize(k_ref[:, cols], k_gain)
        prob = softmax(q_norm, k_norm)
        prob_low = prob.astype(jnp.bfloat16)
        attn = product(prob_low, value, 1, 0).astype(jnp.bfloat16)
        grad = one_ref[:, cols].astype(jnp.float32) + two_ref[:, cols].astype(jnp.float32)
        grad = grad.astype(jnp.bfloat16)
        vg_ref[:, cols] = product(prob_low, grad, 0, 0).astype(jnp.bfloat16)
        delta = jnp.sum(
            grad.astype(jnp.float32) * attn.astype(jnp.float32), axis=-1, keepdims=True
        )
        score_grad = (prob * (product(grad, value, 1, 1) - delta)).astype(jnp.bfloat16)
        qn_grad = product(score_grad, k_norm, 1, 0) * SCALE
        kn_grad = product(score_grad, q_norm, 0, 0) * SCALE
        terms_ref[0:1, :] += jnp.sum(qn_grad * q_unit, axis=0, keepdims=True)
        terms_ref[1:2, :] += jnp.sum(kn_grad * k_unit, axis=0, keepdims=True)
        qg_ref[:, cols] = unnormalize(qn_grad, q_unit, q_inverse, q_gain).astype(jnp.bfloat16)
        kg_ref[:, cols] = unnormalize(kn_grad, k_unit, k_inverse, k_gain).astype(jnp.bfloat16)


def backward(queries_raw, keys_raw, values, part_one, part_two, norm_gains):
    tokens, width = queries_raw.shape
    block = pl.BlockSpec((PATCH, width), lambda i: (i, 0))
    gains = pl.BlockSpec((2, HD), lambda i: (0, 0))
    out = jax.ShapeDtypeStruct((tokens, width), jnp.bfloat16)
    return pl.pallas_call(
        backward_kernel,
        grid=(tokens // PATCH,),
        in_specs=[block] * 5 + [gains],
        out_specs=[block, block, block, gains],
        out_shape=[out, out, out, jax.ShapeDtypeStruct((2, HD), jnp.float32)],
        compiler_params=pltpu.CompilerParams(vmem_limit_bytes=VMEM_LIMIT),
    )(queries_raw, keys_raw, values, part_one, part_two, norm_gains)


def weight_kernel(high_ref, grad_ref, same_ref, other_ref, wgrad_ref):
    high = high_ref[0]
    width = grad_ref.shape[4]
    for core in range(2):
        term = product(grad_ref[high, 0, core], same_ref[...], 0, 0)
        term += product(grad_ref[1 - high, 0, core], other_ref[...], 0, 0)
        wgrad_ref[core * width : (core + 1) * width] = term.astype(wgrad_ref.dtype)


def grad_block(grads):
    return pl.BlockSpec((2, 1) + grads.shape[2:], lambda x, high: (0, x, 0, 0, 0))


def weight_product(high, grads, attn_same, attn_other):
    _, blocks, cores, tokens, width = grads.shape
    heads = attn_same.shape[1]
    attn = pl.BlockSpec((tokens, heads), lambda x, high: (0, 0))
    return pl.pallas_call(
        weight_kernel,
        grid_spec=pltpu.PrefetchScalarGridSpec(
            num_scalar_prefetch=1,
            grid=(blocks,),
            in_specs=[grad_block(grads), attn, attn],
            out_specs=pl.BlockSpec((cores * width, heads), lambda x, high: (x, 0)),
        ),
        out_shape=jax.ShapeDtypeStruct((blocks * cores * width, heads), jnp.bfloat16),
        compiler_params=pltpu.CompilerParams(vmem_limit_bytes=VMEM_LIMIT),
        cost_estimate=pl.CostEstimate(
            flops=2 * grads.size * heads,
            bytes_accessed=2 * (grads.size + blocks * cores * width * heads),
            transcendentals=0,
        ),
    )(high, grads, attn_same, attn_other)


def token_kernel(high_ref, grad_ref, weight_ref, same_ref, other_ref, total):
    step = pl.program_id(0)
    high = high_ref[0]
    weights = weight_ref[...].reshape(-1, weight_ref.shape[3])
    width = grad_ref.shape[4]

    @pl.when(step == 0)
    def _():
        total[...] = jnp.zeros_like(total)

    for index, low in enumerate((high, 1 - high)):
        term = product(grad_ref[low, 0, 0], weights[:width], 1, 0)
        total[index] += term + product(grad_ref[low, 0, 1], weights[width:], 1, 0)

    @pl.when(step == pl.num_programs(0) - 1)
    def _():
        same_ref[...] = total[0].astype(same_ref.dtype)
        other_ref[...] = total[1].astype(other_ref.dtype)


def token_product(high, grads, weights):
    _, blocks, _, tokens, _ = grads.shape
    fours, _, rows, heads = weights.shape
    out = jax.ShapeDtypeStruct((tokens, heads), jnp.bfloat16)
    return pl.pallas_call(
        token_kernel,
        grid_spec=pltpu.PrefetchScalarGridSpec(
            num_scalar_prefetch=1,
            grid=(blocks,),
            in_specs=[
                grad_block(grads),
                pl.BlockSpec((fours, 1, rows, heads), lambda x, high: (0, x, 0, 0)),
            ],
            out_specs=[pl.BlockSpec((tokens, heads), lambda x, high: (0, 0))] * 2,
            scratch_shapes=[pltpu.VMEM((2, tokens, heads), jnp.float32)],
        ),
        out_shape=[out, out],
        compiler_params=pltpu.CompilerParams(vmem_limit_bytes=VMEM_LIMIT),
        cost_estimate=pl.CostEstimate(
            flops=2 * grads.size * heads,
            bytes_accessed=2 * (grads.size + weights.size),
            transcendentals=0,
        ),
    )(high, grads, weights)


def swap_y(array, target):
    pairs = []
    for low in range(2):
        for high in range(2):
            to_low, to_high = target(low, high)
            pairs.append((low * 2 + high, to_low * 2 + to_high))
    return lax.ppermute(array, ("yl", "yh"), pairs)


def turned(array):
    return swap_y(array, lambda low, high: (high, low))


def along(array, step):
    return lax.ppermute(array, Z, [(z, (z + step) % 16) for z in range(16)])


def gather_rows(own_rows):
    column = lax.all_gather(own_rows, "za", axis=0)
    before = along(column, 1)
    after = along(column, -1)
    far = jnp.concatenate([along(column[:2], 2), along(column[2:], -2)])
    blocks = [column, after, far, before]
    shift = (4 - lax.axis_index("zb")) % 4
    return lax.dynamic_slice_in_dim(jnp.stack(blocks + blocks), shift, 4, axis=0)


def sum_over(array, axis, count):
    spread = lax.all_to_all(jnp.broadcast_to(array[None], (count,) + array.shape), axis, 0, 0)
    return jnp.sum(spread, axis=0)


def per_device(queries_raw, keys_raw, values, grad_out, out_weight, norm_gains):
    high = lax.axis_index("yh").reshape(1)
    grads = lax.all_gather(grad_out, ("yl", "x", "c"), axis=0)
    grads = grads.reshape((2, 4, 2) + grad_out.shape)

    attn = forward(queries_raw, keys_raw, values, norm_gains)
    attn_same = turned(attn)
    attn_other = swap_y(attn, lambda low, up: (up, 1 - low))
    weights = gather_rows(turned(out_weight))
    grads, weights = lax.optimization_barrier((grads, weights))

    wgrad = weight_product(high, grads, attn_same, attn_other)
    shard = lax.psum_scatter(wgrad, Z, scatter_dimension=0, tiled=True)

    weights, _ = lax.optimization_barrier((weights, wgrad))
    part_same, part_other = token_product(high, grads, weights)
    came_same = turned(part_same)
    came_other = swap_y(part_other, lambda low, up: (1 - up, low))
    queries_grad, keys_grad, values_grad, terms = backward(
        queries_raw, keys_raw, values, came_same, came_other, norm_gains
    )
    gains_grad = sum_over(sum_over(terms, ("yl", "yh", "x", "c"), 32), Z, 16)
    shard, gains_grad = lax.optimization_barrier((shard, gains_grad))
    weight_grad = turned(shard).astype(jnp.float32)
    return (queries_grad, keys_grad, values_grad, weight_grad, gains_grad)


def solution(mesh):
    fine = Mesh(mesh.devices.reshape(SIZES), AXES)
    spec = P(("yl", "za", "zb"), ("yh", "x", "c"))
    return jax.shard_map(
        per_device,
        mesh=fine,
        in_specs=(spec, spec, spec, spec, spec, P()),
        out_specs=(spec, spec, spec, spec, P()),
        check_vma=False,
    )
```

```python
import jax
import jax.numpy as jnp
from jax import lax
from jax.experimental import pallas as pl
from jax.experimental.pallas import tpu as pltpu
from jax.sharding import Mesh, PartitionSpec as P

HD = 128
PATCH = 256
EPSILON = 1e-06
SCALE = HD ** (-0.5)
AXES = ("yl", "z", "yh", "x", "c")
SIZES = (2, 16, 2, 4, 2)
VMEM_LIMIT = 56 * 1024 * 1024


def normalize(raw, gain):
    values32 = raw.astype(jnp.float32)
    center = values32 - jnp.mean(values32, axis=-1, keepdims=True)
    inverse = lax.rsqrt(jnp.mean(center * center, axis=-1, keepdims=True) + EPSILON)
    unit = center * inverse
    return (unit, inverse, (unit * gain).astype(jnp.bfloat16))


def unnormalize(grad, unit, inverse, gain):
    scaled = grad * gain
    centered = scaled - jnp.mean(scaled, axis=-1, keepdims=True)
    return (centered - unit * jnp.mean(scaled * unit, axis=-1, keepdims=True)) * inverse


def product(left, right, left_dim, right_dim):
    return lax.dot_general(
        left, right, (((left_dim,), (right_dim,)), ((), ())), preferred_element_type=jnp.float32
    )


def softmax(q_norm, k_norm):
    scores = product(q_norm, k_norm, 1, 1) * SCALE
    expo = jnp.exp(scores - jnp.max(scores, axis=-1, keepdims=True))
    return expo / jnp.sum(expo, axis=-1, keepdims=True)


def forward_kernel(q_ref, k_ref, v_ref, gains_ref, attn_ref):
    for head in range(q_ref.shape[1] // HD):
        cols = slice(head * HD, (head + 1) * HD)
        _, _, q_norm = normalize(q_ref[:, cols], gains_ref[0:1, :])
        _, _, k_norm = normalize(k_ref[:, cols], gains_ref[1:2, :])
        prob_low = softmax(q_norm, k_norm).astype(jnp.bfloat16)
        attn_ref[:, cols] = product(prob_low, v_ref[:, cols], 1, 0).astype(jnp.bfloat16)


def forward(queries_raw, keys_raw, values, norm_gains):
    tokens, width = queries_raw.shape
    block = pl.BlockSpec((PATCH, width), lambda i: (i, 0))
    return pl.pallas_call(
        forward_kernel,
        grid=(tokens // PATCH,),
        in_specs=[block, block, block, pl.BlockSpec((2, HD), lambda i: (0, 0))],
        out_specs=block,
        out_shape=jax.ShapeDtypeStruct((tokens, width), jnp.bfloat16),
        compiler_params=pltpu.CompilerParams(vmem_limit_bytes=VMEM_LIMIT),
    )(queries_raw, keys_raw, values, norm_gains)


def backward_kernel(
    q_ref, k_ref, v_ref, one_ref, two_ref, gains_ref, qg_ref, kg_ref, vg_ref, terms_ref
):
    @pl.when(pl.program_id(0) == 0)
    def _():
        terms_ref[...] = jnp.zeros_like(terms_ref)

    q_gain, k_gain = gains_ref[0:1, :], gains_ref[1:2, :]
    for head in range(q_ref.shape[1] // HD):
        cols = slice(head * HD, (head + 1) * HD)
        value = v_ref[:, cols]
        q_unit, q_inverse, q_norm = normalize(q_ref[:, cols], q_gain)
        k_unit, k_inverse, k_norm = normalize(k_ref[:, cols], k_gain)
        prob = softmax(q_norm, k_norm)
        prob_low = prob.astype(jnp.bfloat16)
        attn = product(prob_low, value, 1, 0).astype(jnp.bfloat16)
        grad = one_ref[:, cols].astype(jnp.float32) + two_ref[:, cols].astype(jnp.float32)
        grad = grad.astype(jnp.bfloat16)
        vg_ref[:, cols] = product(prob_low, grad, 0, 0).astype(jnp.bfloat16)
        delta = jnp.sum(
            grad.astype(jnp.float32) * attn.astype(jnp.float32), axis=-1, keepdims=True
        )
        score_grad = (prob * (product(grad, value, 1, 1) - delta)).astype(jnp.bfloat16)
        qn_grad = product(score_grad, k_norm, 1, 0) * SCALE
        kn_grad = product(score_grad, q_norm, 0, 0) * SCALE
        terms_ref[0:1, :] += jnp.sum(qn_grad * q_unit, axis=0, keepdims=True)
        terms_ref[1:2, :] += jnp.sum(kn_grad * k_unit, axis=0, keepdims=True)
        qg_ref[:, cols] = unnormalize(qn_grad, q_unit, q_inverse, q_gain).astype(jnp.bfloat16)
        kg_ref[:, cols] = unnormalize(kn_grad, k_unit, k_inverse, k_gain).astype(jnp.bfloat16)


def backward(queries_raw, keys_raw, values, part_one, part_two, norm_gains):
    tokens, width = queries_raw.shape
    block = pl.BlockSpec((PATCH, width), lambda i: (i, 0))
    gains = pl.BlockSpec((2, HD), lambda i: (0, 0))
    out = jax.ShapeDtypeStruct((tokens, width), jnp.bfloat16)
    return pl.pallas_call(
        backward_kernel,
        grid=(tokens // PATCH,),
        in_specs=[block] * 5 + [gains],
        out_specs=[block, block, block, gains],
        out_shape=[out, out, out, jax.ShapeDtypeStruct((2, HD), jnp.float32)],
        compiler_params=pltpu.CompilerParams(vmem_limit_bytes=VMEM_LIMIT),
    )(queries_raw, keys_raw, values, part_one, part_two, norm_gains)


STEPS = (0, 3, 1, 2)
CHUNK = 256


def row_block(place_ref, index):
    x = lax.rem(place_ref[0] + STEPS[index % 4], 4)
    core = place_ref[1] if index < 4 else 1 - place_ref[1]
    return 2 * x + core


def rows_of(place_ref, index, width):
    return pl.ds(pl.multiple_of(row_block(place_ref, index) * width, width), width)


def weight_kernel(place_ref, own_attn_ref, other_attn_ref, *refs):
    own_refs, other_refs, (wgrad_ref, total) = refs[:8], refs[8:16], refs[16:]
    step = pl.program_id(0)
    width = own_refs[0].shape[1]
    own_attn, other_attn = own_attn_ref[...], other_attn_ref[...]
    for index in range(8):
        rows = rows_of(place_ref, index, width)
        term = product(own_refs[index][...], own_attn, 0, 0)
        term += product(other_refs[index][...], other_attn, 0, 0)

        @pl.when(step == 0)
        def _():
            total[rows] = term

        @pl.when(step > 0)
        def _():
            total[rows] += term

    @pl.when(step == pl.num_programs(0) - 1)
    def _():
        wgrad_ref[...] = total[...].astype(wgrad_ref.dtype)


def weight_product(place, own, other, own_attn, other_attn):
    tokens, width = own[0].shape
    heads = own_attn.shape[1]
    rows = 8 * width
    block = pl.BlockSpec((CHUNK, width), lambda i, place: (i, 0))
    attn = pl.BlockSpec((CHUNK, heads), lambda i, place: (i, 0))
    return pl.pallas_call(
        weight_kernel,
        grid_spec=pltpu.PrefetchScalarGridSpec(
            num_scalar_prefetch=1,
            grid=(tokens // CHUNK,),
            in_specs=[attn, attn] + [block] * 16,
            out_specs=pl.BlockSpec((rows, heads), lambda i, place: (0, 0)),
            scratch_shapes=[pltpu.VMEM((rows, heads), jnp.float32)],
        ),
        out_shape=jax.ShapeDtypeStruct((rows, heads), jnp.bfloat16),
        compiler_params=pltpu.CompilerParams(vmem_limit_bytes=VMEM_LIMIT),
        cost_estimate=pl.CostEstimate(
            flops=4 * rows * tokens * heads,
            bytes_accessed=2 * (2 * rows * tokens + rows * heads),
            transcendentals=0,
        ),
    )(place, own_attn, other_attn, *own, *other)


def token_kernel(place_ref, weight_ref, *refs):
    blocks, part_ref = refs[:8], refs[8]
    width = blocks[0].shape[1]
    total = None
    for index in range(8):
        term = product(blocks[index][...], weight_ref[rows_of(place_ref, index, width)], 1, 0)
        total = term if total is None else total + term
    part_ref[...] = total.astype(part_ref.dtype)


def token_product(place, blocks, weights):
    tokens, width = blocks[0].shape
    rows, heads = weights.shape
    return pl.pallas_call(
        token_kernel,
        grid_spec=pltpu.PrefetchScalarGridSpec(
            num_scalar_prefetch=1,
            grid=(tokens // CHUNK,),
            in_specs=[pl.BlockSpec((rows, heads), lambda i, place: (0, 0))]
            + [pl.BlockSpec((CHUNK, width), lambda i, place: (i, 0))] * 8,
            out_specs=pl.BlockSpec((CHUNK, heads), lambda i, place: (i, 0)),
        ),
        out_shape=jax.ShapeDtypeStruct((tokens, heads), jnp.bfloat16),
        compiler_params=pltpu.CompilerParams(vmem_limit_bytes=VMEM_LIMIT),
        cost_estimate=pl.CostEstimate(
            flops=2 * rows * tokens * heads,
            bytes_accessed=2 * rows * (tokens + heads),
            transcendentals=0,
        ),
    )(place, weights, *blocks)


def swap_y(array, target):
    pairs = []
    for low in range(2):
        for high in range(2):
            place = target(low, high)
            if place is not None:
                pairs.append((low * 2 + high, place[0] * 2 + place[1]))
    return lax.ppermute(array, ("yl", "yh"), pairs)


def to_partner(array):
    return lax.ppermute(array, "yl", [(0, 1), (1, 0)])


def to_core(array):
    return lax.ppermute(array, "c", [(0, 1), (1, 0)])


def along_x(array, step):
    return lax.ppermute(array, "x", [(x, (x + step) % 4) for x in range(4)])


def halves_for(grad_out):
    near = swap_y(grad_out, lambda low, up: (up, up) if low != up else None)
    cross = swap_y(grad_out, lambda low, up: (up, 1 - up) if low != up else None)
    far = swap_y(grad_out, lambda low, up: (up, 1 - up) if low == up else None)
    stays = lax.axis_index("yl") == lax.axis_index("yh")
    return jnp.where(stays, grad_out, far), jnp.where(stays, near, cross)


def round_x(block):
    half = block.shape[0] // 2
    left, right = along_x(block, 1), along_x(block, -1)
    opposite = [along_x(left[:half], 1), along_x(right[half:], -1)]
    blocks = [block, left, right, jnp.concatenate(opposite)]
    return blocks + [to_core(piece) for piece in blocks]


def sum_over(array, axis, count):
    spread = lax.all_to_all(jnp.broadcast_to(array[None], (count,) + array.shape), axis, 0, 0)
    return jnp.sum(spread, axis=0)


def per_device(queries_raw, keys_raw, values, grad_out, out_weight, norm_gains):
    place = jnp.stack([lax.axis_index("x"), lax.axis_index("c")]).astype(jnp.int32)
    weights = lax.all_gather(out_weight, "z", axis=0, tiled=True)
    own, other = halves_for(grad_out)
    other, own = round_x(other), round_x(own)

    attn = forward(queries_raw, keys_raw, values, norm_gains)
    wgrad = weight_product(place, own, other, attn, to_partner(attn))
    shard = lax.psum_scatter(wgrad, "z", scatter_dimension=0, tiled=True)

    weights, _ = lax.optimization_barrier((weights, wgrad))
    part_other = token_product(place, other, weights)
    weights, _ = lax.optimization_barrier((weights, part_other))
    part_own = token_product(place, own, weights)
    queries_grad, keys_grad, values_grad, terms = backward(
        queries_raw, keys_raw, values, part_own, to_partner(part_other), norm_gains
    )
    gains_grad = sum_over(sum_over(terms, ("yl", "yh", "x", "c"), 32), "z", 16)
    shard, gains_grad = lax.optimization_barrier((shard, gains_grad))
    return (queries_grad, keys_grad, values_grad, shard.astype(jnp.float32), gains_grad)


def solution(mesh):
    fine = Mesh(mesh.devices.reshape(SIZES), AXES)
    spec = P(("yl", "z"), ("yh", "x", "c"))
    return jax.shard_map(
        per_device,
        mesh=fine,
        in_specs=(spec, spec, spec, spec, spec, P()),
        out_specs=(spec, spec, spec, spec, P()),
        check_vma=False,
    )
```

```python
import jax
import jax.numpy as jnp
from jax import lax
from jax.experimental import pallas as pl
from jax.experimental.pallas import tpu as pltpu
from jax.sharding import Mesh, PartitionSpec as P

HD = 128
PATCH = 256
EPSILON = 1e-06
SCALE = HD ** (-0.5)
AXES = ("yl", "zp", "zq", "zb", "yh", "xp", "xq", "c")
SIZES = (2, 2, 2, 4, 2, 2, 2, 2)
Z = ("zp", "zq", "zb")
VMEM_LIMIT = 56 * 1024 * 1024


def normalize(raw, gain):
    values32 = raw.astype(jnp.float32)
    center = values32 - jnp.mean(values32, axis=-1, keepdims=True)
    inverse = lax.rsqrt(jnp.mean(center * center, axis=-1, keepdims=True) + EPSILON)
    unit = center * inverse
    return (unit, inverse, (unit * gain).astype(jnp.bfloat16))


def unnormalize(grad, unit, inverse, gain):
    scaled = grad * gain
    centered = scaled - jnp.mean(scaled, axis=-1, keepdims=True)
    return (centered - unit * jnp.mean(scaled * unit, axis=-1, keepdims=True)) * inverse


def product(left, right, left_dim, right_dim):
    return lax.dot_general(
        left, right, (((left_dim,), (right_dim,)), ((), ())), preferred_element_type=jnp.float32
    )


def softmax(q_norm, k_norm):
    scores = product(q_norm, k_norm, 1, 1) * SCALE
    expo = jnp.exp(scores - jnp.max(scores, axis=-1, keepdims=True))
    return expo / jnp.sum(expo, axis=-1, keepdims=True)


def forward_kernel(q_ref, k_ref, v_ref, gains_ref, attn_ref):
    for head in range(q_ref.shape[1] // HD):
        cols = slice(head * HD, (head + 1) * HD)
        _, _, q_norm = normalize(q_ref[:, cols], gains_ref[0:1, :])
        _, _, k_norm = normalize(k_ref[:, cols], gains_ref[1:2, :])
        prob_low = softmax(q_norm, k_norm).astype(jnp.bfloat16)
        attn_ref[:, cols] = product(prob_low, v_ref[:, cols], 1, 0).astype(jnp.bfloat16)


def forward(queries_raw, keys_raw, values, norm_gains):
    tokens, width = queries_raw.shape
    block = pl.BlockSpec((PATCH, width), lambda i: (i, 0))
    return pl.pallas_call(
        forward_kernel,
        grid=(tokens // PATCH,),
        in_specs=[block, block, block, pl.BlockSpec((2, HD), lambda i: (0, 0))],
        out_specs=block,
        out_shape=jax.ShapeDtypeStruct((tokens, width), jnp.bfloat16),
        compiler_params=pltpu.CompilerParams(vmem_limit_bytes=VMEM_LIMIT),
    )(queries_raw, keys_raw, values, norm_gains)


def backward_kernel(
    q_ref, k_ref, v_ref, p0_ref, p1_ref, p2_ref, p3_ref, gains_ref,
    qg_ref, kg_ref, vg_ref, terms_ref,
):
    @pl.when(pl.program_id(0) == 0)
    def _():
        terms_ref[...] = jnp.zeros_like(terms_ref)

    q_gain, k_gain = gains_ref[0:1, :], gains_ref[1:2, :]
    for head in range(q_ref.shape[1] // HD):
        cols = slice(head * HD, (head + 1) * HD)
        value = v_ref[:, cols]
        q_unit, q_inverse, q_norm = normalize(q_ref[:, cols], q_gain)
        k_unit, k_inverse, k_norm = normalize(k_ref[:, cols], k_gain)
        prob = softmax(q_norm, k_norm)
        prob_low = prob.astype(jnp.bfloat16)
        attn = product(prob_low, value, 1, 0).astype(jnp.bfloat16)
        grad = sum(ref[:, cols].astype(jnp.float32) for ref in (p0_ref, p1_ref, p2_ref, p3_ref))
        grad = grad.astype(jnp.bfloat16)
        vg_ref[:, cols] = product(prob_low, grad, 0, 0).astype(jnp.bfloat16)
        delta = jnp.sum(
            grad.astype(jnp.float32) * attn.astype(jnp.float32), axis=-1, keepdims=True
        )
        score_grad = (prob * (product(grad, value, 1, 1) - delta)).astype(jnp.bfloat16)
        qn_grad = product(score_grad, k_norm, 1, 0) * SCALE
        kn_grad = product(score_grad, q_norm, 0, 0) * SCALE
        terms_ref[0:1, :] += jnp.sum(qn_grad * q_unit, axis=0, keepdims=True)
        terms_ref[1:2, :] += jnp.sum(kn_grad * k_unit, axis=0, keepdims=True)
        qg_ref[:, cols] = unnormalize(qn_grad, q_unit, q_inverse, q_gain).astype(jnp.bfloat16)
        kg_ref[:, cols] = unnormalize(kn_grad, k_unit, k_inverse, k_gain).astype(jnp.bfloat16)


def backward(queries_raw, keys_raw, values, parts, norm_gains):
    tokens, width = queries_raw.shape
    block = pl.BlockSpec((PATCH, width), lambda i: (i, 0))
    gains = pl.BlockSpec((2, HD), lambda i: (0, 0))
    out = jax.ShapeDtypeStruct((tokens, width), jnp.bfloat16)
    return pl.pallas_call(
        backward_kernel,
        grid=(tokens // PATCH,),
        in_specs=[block] * 7 + [gains],
        out_specs=[block, block, block, gains],
        out_shape=[out, out, out, jax.ShapeDtypeStruct((2, HD), jnp.float32)],
        compiler_params=pltpu.CompilerParams(vmem_limit_bytes=VMEM_LIMIT),
    )(queries_raw, keys_raw, values, *parts, norm_gains)


def grad_block(grads):
    return pl.BlockSpec((2, 1, 1) + grads.shape[3:], lambda x, c, place: (0, x, c, 0, 0))


def weight_kernel(place_ref, grad_ref, same_ref, other_ref, wgrad_ref):
    high, mine = place_ref[0], place_ref[1]
    heads = wgrad_ref.shape[3]
    term = product(grad_ref[high, 0, 0], same_ref[...], 0, 0)
    term += product(grad_ref[1 - high, 0, 0], other_ref[...], 0, 0)
    term = term.astype(wgrad_ref.dtype)
    wgrad_ref[0, mine] = term[:, :heads]
    wgrad_ref[0, 1 - mine] = term[:, heads:]


def weight_product(place, grads, attn_same, attn_other):
    _, _, _, tokens, width = grads.shape
    heads = attn_same.shape[1] // 2
    attn = pl.BlockSpec((tokens, 2 * heads), lambda x, c, place: (0, 0))
    return pl.pallas_call(
        weight_kernel,
        grid_spec=pltpu.PrefetchScalarGridSpec(
            num_scalar_prefetch=1,
            grid=(2, 2),
            in_specs=[grad_block(grads), attn, attn],
            out_specs=pl.BlockSpec((1, 2, width, heads), lambda x, c, place: (x, 0, c, 0)),
        ),
        out_shape=jax.ShapeDtypeStruct((2, 2, 2 * width, heads), jnp.bfloat16),
        compiler_params=pltpu.CompilerParams(vmem_limit_bytes=VMEM_LIMIT),
        cost_estimate=pl.CostEstimate(
            flops=4 * grads.size * heads,
            bytes_accessed=2 * (grads.size + 8 * width * heads),
            transcendentals=0,
        ),
    )(place, grads, attn_same, attn_other)


def token_kernel(place_ref, grad_ref, weight_ref, *refs):
    parts, total = refs[:4], refs[4]
    step = 2 * pl.program_id(0) + pl.program_id(1)
    high, mine = place_ref[0], place_ref[1]

    @pl.when(step == 0)
    def _():
        total[...] = jnp.zeros_like(total)

    for side, column in enumerate((mine, 1 - mine)):
        weights = weight_ref[:, 0, column].reshape(-1, weight_ref.shape[4])
        for index, low in enumerate((high, 1 - high)):
            total[2 * index + side] += product(grad_ref[low, 0, 0], weights, 1, 0)

    @pl.when(step == 3)
    def _():
        for index in range(4):
            parts[index][...] = total[index].astype(parts[index].dtype)


def token_product(place, grads, weights):
    _, _, _, tokens, _ = grads.shape
    rows, heads = weights.shape[3:]
    return pl.pallas_call(
        token_kernel,
        grid_spec=pltpu.PrefetchScalarGridSpec(
            num_scalar_prefetch=1,
            grid=(2, 2),
            in_specs=[
                grad_block(grads),
                pl.BlockSpec((2, 1, 2, rows, heads), lambda x, c, place: (c, x, 0, 0, 0)),
            ],
            out_specs=[pl.BlockSpec((tokens, heads), lambda x, c, place: (0, 0))] * 4,
            scratch_shapes=[pltpu.VMEM((4, tokens, heads), jnp.float32)],
        ),
        out_shape=[jax.ShapeDtypeStruct((tokens, heads), jnp.bfloat16)] * 4,
        compiler_params=pltpu.CompilerParams(vmem_limit_bytes=VMEM_LIMIT),
        cost_estimate=pl.CostEstimate(
            flops=4 * grads.size * heads,
            bytes_accessed=2 * (grads.size + weights.size),
            transcendentals=0,
        ),
    )(place, grads, weights)


def permute(array, axes, target):
    count = len(axes)
    pairs = []
    for source in range(2**count):
        place = [(source >> (count - 1 - i)) & 1 for i in range(count)]
        goal = 0
        for value in target(*place):
            goal = 2 * goal + value % 2
        pairs.append((source, goal))
    return lax.ppermute(array, axes, pairs)


def exchanged(array):
    return permute(
        array,
        ("yl", "zq", "yh", "xq"),
        lambda low, zq, up, xq: (up, zq + (zq != xq), low, xq + (zq != xq)),
    )


def along(array, step):
    return lax.ppermute(array, Z, [(z, (z + step) % 16) for z in range(16)])


def gather_rows(own_rows):
    column = lax.all_gather(own_rows, ("zp", "zq"), axis=0)
    before = along(column, 1)
    after = along(column, -1)
    far = jnp.concatenate([along(column[:2], 2), along(column[2:], -2)])
    blocks = [column, after, far, before]
    shift = (4 - lax.axis_index("zb")) % 4
    rows = lax.dynamic_slice_in_dim(jnp.stack(blocks + blocks), shift, 4, axis=0)
    return rows.reshape((4, 2, 2) + own_rows.shape)


def sum_over(array, axis, count):
    spread = lax.all_to_all(jnp.broadcast_to(array[None], (count,) + array.shape), axis, 0, 0)
    return jnp.sum(spread, axis=0)


def per_device(queries_raw, keys_raw, values, grad_out, out_weight, norm_gains):
    place = jnp.stack([lax.axis_index("yh"), lax.axis_index("xq")]).astype(jnp.int32)
    grads = lax.all_gather(grad_out, ("yl", "xp", "c"), axis=0)
    grads = grads.reshape((2, 2, 2) + grad_out.shape)

    attn = forward(queries_raw, keys_raw, values, norm_gains)
    own_rows, attn = lax.optimization_barrier((exchanged(out_weight), attn))
    weights = gather_rows(own_rows)
    beside = permute(attn, ("xq",), lambda xq: (1 - xq,))
    attn = jnp.concatenate([attn, beside], axis=1)
    attn_same = permute(attn, ("yl", "yh"), lambda low, up: (up, low))
    attn_other = permute(attn, ("yl", "yh"), lambda low, up: (up, 1 - low))
    grads, weights = lax.optimization_barrier((grads, weights))

    wgrad = weight_product(place, grads, attn_same, attn_other)
    shard = lax.psum_scatter(
        wgrad.reshape(-1, wgrad.shape[3]), Z, scatter_dimension=0, tiled=True
    )

    weights, _ = lax.optimization_barrier((weights, wgrad))
    same, same_beside, other, other_beside = token_product(place, grads, weights)
    axes = ("yl", "yh", "xq")
    parts = [
        permute(same, axes, lambda low, up, xq: (up, low, xq)),
        permute(same_beside, axes, lambda low, up, xq: (up, low, 1 - xq)),
        permute(other, axes, lambda low, up, xq: (1 - up, low, xq)),
        permute(other_beside, axes, lambda low, up, xq: (1 - up, low, 1 - xq)),
    ]
    queries_grad, keys_grad, values_grad, terms = backward(
        queries_raw, keys_raw, values, parts, norm_gains
    )
    gains_grad = sum_over(sum_over(terms, ("yl", "yh", "xp", "xq", "c"), 32), Z, 16)
    shard, gains_grad = lax.optimization_barrier((shard, gains_grad))
    weight_grad = exchanged(shard).astype(jnp.float32)
    return (queries_grad, keys_grad, values_grad, weight_grad, gains_grad)


def solution(mesh):
    fine = Mesh(mesh.devices.reshape(SIZES), AXES)
    spec = P(("yl", "zp", "zq", "zb"), ("yh", "xp", "xq", "c"))
    return jax.shard_map(
        per_device,
        mesh=fine,
        in_specs=(spec, spec, spec, spec, spec, P()),
        out_specs=(spec, spec, spec, spec, P()),
        check_vma=False,
    )
```

```python
import jax
import jax.numpy as jnp
from jax import lax
from jax.experimental import pallas as pl
from jax.experimental.pallas import tpu as pltpu
from jax.sharding import Mesh, PartitionSpec as P

HD = 128
PATCH = 256
EPSILON = 1e-06
SCALE = HD ** (-0.5)
AXES = ("yl", "zp", "zq", "zb", "yh", "xp", "xq", "c")
SIZES = (2, 2, 2, 4, 2, 2, 2, 2)
Z = ("zp", "zq", "zb")
VMEM_LIMIT = 56 * 1024 * 1024


def normalize(raw, gain):
    values32 = raw.astype(jnp.float32)
    center = values32 - jnp.mean(values32, axis=-1, keepdims=True)
    inverse = lax.rsqrt(jnp.mean(center * center, axis=-1, keepdims=True) + EPSILON)
    unit = center * inverse
    return (unit, inverse, (unit * gain).astype(jnp.bfloat16))


def unnormalize(grad, unit, inverse, gain):
    scaled = grad * gain
    centered = scaled - jnp.mean(scaled, axis=-1, keepdims=True)
    return (centered - unit * jnp.mean(scaled * unit, axis=-1, keepdims=True)) * inverse


def product(left, right, left_dim, right_dim):
    return lax.dot_general(
        left, right, (((left_dim,), (right_dim,)), ((), ())), preferred_element_type=jnp.float32
    )


def softmax(q_norm, k_norm):
    scores = product(q_norm, k_norm, 1, 1) * SCALE
    expo = jnp.exp(scores - jnp.max(scores, axis=-1, keepdims=True))
    return expo / jnp.sum(expo, axis=-1, keepdims=True)


def forward_kernel(q_ref, k_ref, v_ref, gains_ref, attn_ref):
    for head in range(q_ref.shape[1] // HD):
        cols = slice(head * HD, (head + 1) * HD)
        _, _, q_norm = normalize(q_ref[:, cols], gains_ref[0:1, :])
        _, _, k_norm = normalize(k_ref[:, cols], gains_ref[1:2, :])
        prob_low = softmax(q_norm, k_norm).astype(jnp.bfloat16)
        attn_ref[:, cols] = product(prob_low, v_ref[:, cols], 1, 0).astype(jnp.bfloat16)


def forward(queries_raw, keys_raw, values, norm_gains):
    tokens, width = queries_raw.shape
    block = pl.BlockSpec((PATCH, width), lambda i: (i, 0))
    return pl.pallas_call(
        forward_kernel,
        grid=(tokens // PATCH,),
        in_specs=[block, block, block, pl.BlockSpec((2, HD), lambda i: (0, 0))],
        out_specs=block,
        out_shape=jax.ShapeDtypeStruct((tokens, width), jnp.bfloat16),
        compiler_params=pltpu.CompilerParams(vmem_limit_bytes=VMEM_LIMIT),
    )(queries_raw, keys_raw, values, norm_gains)


def backward_kernel(
    q_ref, k_ref, v_ref, p0_ref, p1_ref, p2_ref, p3_ref, gains_ref,
    qg_ref, kg_ref, vg_ref, terms_ref,
):
    @pl.when(pl.program_id(0) == 0)
    def _():
        terms_ref[...] = jnp.zeros_like(terms_ref)

    q_gain, k_gain = gains_ref[0:1, :], gains_ref[1:2, :]
    for head in range(q_ref.shape[1] // HD):
        cols = slice(head * HD, (head + 1) * HD)
        value = v_ref[:, cols]
        q_unit, q_inverse, q_norm = normalize(q_ref[:, cols], q_gain)
        k_unit, k_inverse, k_norm = normalize(k_ref[:, cols], k_gain)
        prob = softmax(q_norm, k_norm)
        prob_low = prob.astype(jnp.bfloat16)
        attn = product(prob_low, value, 1, 0).astype(jnp.bfloat16)
        grad = sum(ref[:, cols].astype(jnp.float32) for ref in (p0_ref, p1_ref, p2_ref, p3_ref))
        grad = grad.astype(jnp.bfloat16)
        vg_ref[:, cols] = product(prob_low, grad, 0, 0).astype(jnp.bfloat16)
        delta = jnp.sum(
            grad.astype(jnp.float32) * attn.astype(jnp.float32), axis=-1, keepdims=True
        )
        score_grad = (prob * (product(grad, value, 1, 1) - delta)).astype(jnp.bfloat16)
        qn_grad = product(score_grad, k_norm, 1, 0) * SCALE
        kn_grad = product(score_grad, q_norm, 0, 0) * SCALE
        terms_ref[0:1, :] += jnp.sum(qn_grad * q_unit, axis=0, keepdims=True)
        terms_ref[1:2, :] += jnp.sum(kn_grad * k_unit, axis=0, keepdims=True)
        qg_ref[:, cols] = unnormalize(qn_grad, q_unit, q_inverse, q_gain).astype(jnp.bfloat16)
        kg_ref[:, cols] = unnormalize(kn_grad, k_unit, k_inverse, k_gain).astype(jnp.bfloat16)


def backward(queries_raw, keys_raw, values, parts, norm_gains):
    tokens, width = queries_raw.shape
    block = pl.BlockSpec((PATCH, width), lambda i: (i, 0))
    gains = pl.BlockSpec((2, HD), lambda i: (0, 0))
    out = jax.ShapeDtypeStruct((tokens, width), jnp.bfloat16)
    return pl.pallas_call(
        backward_kernel,
        grid=(tokens // PATCH,),
        in_specs=[block] * 7 + [gains],
        out_specs=[block, block, block, gains],
        out_shape=[out, out, out, jax.ShapeDtypeStruct((2, HD), jnp.float32)],
        compiler_params=pltpu.CompilerParams(vmem_limit_bytes=VMEM_LIMIT),
    )(queries_raw, keys_raw, values, *parts, norm_gains)


def grad_block(grads):
    return pl.BlockSpec((2, 1, 1) + grads.shape[3:], lambda x, c, place: (0, x, c, 0, 0))


def weight_kernel(place_ref, grad_ref, same_ref, other_ref, wgrad_ref):
    high, mine = place_ref[0], place_ref[1]
    heads = wgrad_ref.shape[3]
    term = product(grad_ref[high, 0, 0], same_ref[...], 0, 0)
    term += product(grad_ref[1 - high, 0, 0], other_ref[...], 0, 0)
    term = term.astype(wgrad_ref.dtype)
    wgrad_ref[0, mine] = term[:, :heads]
    wgrad_ref[0, 1 - mine] = term[:, heads:]


def weight_product(place, grads, attn_same, attn_other):
    _, _, _, tokens, width = grads.shape
    heads = attn_same.shape[1] // 2
    attn = pl.BlockSpec((tokens, 2 * heads), lambda x, c, place: (0, 0))
    return pl.pallas_call(
        weight_kernel,
        grid_spec=pltpu.PrefetchScalarGridSpec(
            num_scalar_prefetch=1,
            grid=(2, 2),
            in_specs=[grad_block(grads), attn, attn],
            out_specs=pl.BlockSpec((1, 2, width, heads), lambda x, c, place: (x, 0, c, 0)),
        ),
        out_shape=jax.ShapeDtypeStruct((2, 2, 2 * width, heads), jnp.bfloat16),
        compiler_params=pltpu.CompilerParams(vmem_limit_bytes=VMEM_LIMIT),
        cost_estimate=pl.CostEstimate(
            flops=4 * grads.size * heads,
            bytes_accessed=2 * (grads.size + 8 * width * heads),
            transcendentals=0,
        ),
    )(place, grads, attn_same, attn_other)


def token_kernel(place_ref, grad_ref, weight_ref, *refs):
    parts, total = refs[:4], refs[4]
    step = 2 * pl.program_id(0) + pl.program_id(1)
    high, mine = place_ref[0], place_ref[1]

    @pl.when(step == 0)
    def _():
        total[...] = jnp.zeros_like(total)

    for side, column in enumerate((mine, 1 - mine)):
        weights = weight_ref[:, 0, column].reshape(-1, weight_ref.shape[4])
        for index, low in enumerate((high, 1 - high)):
            total[2 * index + side] += product(grad_ref[low, 0, 0], weights, 1, 0)

    @pl.when(step == 3)
    def _():
        for index in range(4):
            parts[index][...] = total[index].astype(parts[index].dtype)


def token_product(place, grads, weights):
    _, _, _, tokens, _ = grads.shape
    rows, heads = weights.shape[3:]
    return pl.pallas_call(
        token_kernel,
        grid_spec=pltpu.PrefetchScalarGridSpec(
            num_scalar_prefetch=1,
            grid=(2, 2),
            in_specs=[
                grad_block(grads),
                pl.BlockSpec((2, 1, 2, rows, heads), lambda x, c, place: (c, x, 0, 0, 0)),
            ],
            out_specs=[pl.BlockSpec((tokens, heads), lambda x, c, place: (0, 0))] * 4,
            scratch_shapes=[pltpu.VMEM((4, tokens, heads), jnp.float32)],
        ),
        out_shape=[jax.ShapeDtypeStruct((tokens, heads), jnp.bfloat16)] * 4,
        compiler_params=pltpu.CompilerParams(vmem_limit_bytes=VMEM_LIMIT),
        cost_estimate=pl.CostEstimate(
            flops=4 * grads.size * heads,
            bytes_accessed=2 * (grads.size + weights.size),
            transcendentals=0,
        ),
    )(place, grads, weights)


def permute(array, axes, target):
    count = len(axes)
    pairs = []
    for source in range(2**count):
        place = [(source >> (count - 1 - i)) & 1 for i in range(count)]
        goal = 0
        for value in target(*place):
            goal = 2 * goal + value % 2
        pairs.append((source, goal))
    return lax.ppermute(array, axes, pairs)


def rows_to_worker(array):
    return permute(
        array,
        ("yl", "zq", "yh", "xq"),
        lambda low, zq, up, xq: (1 - up, zq + (zq != xq), low, xq + (zq != xq)),
    )


def rows_to_owner(array):
    return permute(
        array,
        ("yl", "zq", "yh", "xq"),
        lambda low, zq, up, xq: (up, zq + (zq != xq), 1 - low, xq + (zq != xq)),
    )


def along(array, step):
    return lax.ppermute(array, Z, [(z, (z + step) % 16) for z in range(16)])


def gather_rows(own_rows):
    column = lax.all_gather(own_rows, ("zp", "zq"), axis=0)
    before = along(column, 1)
    after = along(column, -1)
    far = jnp.concatenate([along(column[:2], 2), along(column[2:], -2)])
    blocks = [column, after, far, before]
    shift = (4 - lax.axis_index("zb")) % 4
    rows = lax.dynamic_slice_in_dim(jnp.stack(blocks + blocks), shift, 4, axis=0)
    return rows.reshape((4, 2, 2) + own_rows.shape)


def sum_over(array, axis, count):
    spread = lax.all_to_all(jnp.broadcast_to(array[None], (count,) + array.shape), axis, 0, 0)
    return jnp.sum(spread, axis=0)


def per_device(queries_raw, keys_raw, values, grad_out, out_weight, norm_gains):
    place = jnp.stack([lax.axis_index("yh"), lax.axis_index("xq")]).astype(jnp.int32)
    grads = lax.all_gather(grad_out, ("yl", "xp", "c"), axis=0)
    grads = grads.reshape((2, 2, 2) + grad_out.shape)

    attn = forward(queries_raw, keys_raw, values, norm_gains)
    beside = permute(attn, ("xq",), lambda xq: (1 - xq,))
    own_rows, beside = lax.optimization_barrier((rows_to_worker(out_weight), beside))
    attn = jnp.concatenate([attn, beside], axis=1)
    attn_same = permute(attn, ("yl", "yh"), lambda low, up: (1 - up, low))
    attn_other = permute(attn, ("yl", "yh"), lambda low, up: (1 - up, 1 - low))
    weights = gather_rows(own_rows)
    grads, weights = lax.optimization_barrier((grads, weights))

    wgrad = weight_product(place, grads, attn_same, attn_other)
    shard = lax.psum_scatter(
        wgrad.reshape(-1, wgrad.shape[3]), Z, scatter_dimension=0, tiled=True
    )

    weights, _ = lax.optimization_barrier((weights, wgrad))
    same, same_beside, other, other_beside = token_product(place, grads, weights)
    axes = ("yl", "yh", "xq")
    parts = [
        permute(same, axes, lambda low, up, xq: (up, 1 - low, xq)),
        permute(same_beside, axes, lambda low, up, xq: (up, 1 - low, 1 - xq)),
        permute(other, axes, lambda low, up, xq: (1 - up, 1 - low, xq)),
        permute(other_beside, axes, lambda low, up, xq: (1 - up, 1 - low, 1 - xq)),
    ]
    queries_grad, keys_grad, values_grad, terms = backward(
        queries_raw, keys_raw, values, parts, norm_gains
    )
    gains_grad = sum_over(sum_over(terms, ("yl", "yh", "xp", "xq", "c"), 32), Z, 16)
    shard, gains_grad = lax.optimization_barrier((shard, gains_grad))
    weight_grad = rows_to_owner(shard).astype(jnp.float32)
    return (queries_grad, keys_grad, values_grad, weight_grad, gains_grad)


def solution(mesh):
    fine = Mesh(mesh.devices.reshape(SIZES), AXES)
    spec = P(("yl", "zp", "zq", "zb"), ("yh", "xp", "xq", "c"))
    return jax.shard_map(
        per_device,
        mesh=fine,
        in_specs=(spec, spec, spec, spec, spec, P()),
        out_specs=(spec, spec, spec, spec, P()),
        check_vma=False,
    )
```

```python
import jax
import jax.numpy as jnp
from jax import lax
from jax.experimental import pallas as pl
from jax.experimental.pallas import tpu as pltpu
from jax.sharding import Mesh, PartitionSpec as P

HD = 128
PATCH = 256
EPSILON = 1e-06
SCALE = HD ** (-0.5)
AXES = ("yl", "z", "yh", "x", "c")
SIZES = (2, 16, 2, 4, 2)
VMEM_LIMIT = 56 * 1024 * 1024


def normalize(raw, gain):
    values32 = raw.astype(jnp.float32)
    center = values32 - jnp.mean(values32, axis=-1, keepdims=True)
    inverse = lax.rsqrt(jnp.mean(center * center, axis=-1, keepdims=True) + EPSILON)
    unit = center * inverse
    return (unit, inverse, (unit * gain).astype(jnp.bfloat16))


def unnormalize(grad, unit, inverse, gain):
    scaled = grad * gain
    centered = scaled - jnp.mean(scaled, axis=-1, keepdims=True)
    return (centered - unit * jnp.mean(scaled * unit, axis=-1, keepdims=True)) * inverse


def product(left, right, left_dim, right_dim):
    return lax.dot_general(
        left, right, (((left_dim,), (right_dim,)), ((), ())), preferred_element_type=jnp.float32
    )


def softmax(q_norm, k_norm):
    scores = product(q_norm, k_norm, 1, 1) * SCALE
    expo = jnp.exp(scores - jnp.max(scores, axis=-1, keepdims=True))
    return expo / jnp.sum(expo, axis=-1, keepdims=True)


def forward_kernel(q_ref, k_ref, v_ref, gains_ref, attn_ref):
    for head in range(q_ref.shape[1] // HD):
        cols = slice(head * HD, (head + 1) * HD)
        _, _, q_norm = normalize(q_ref[:, cols], gains_ref[0:1, :])
        _, _, k_norm = normalize(k_ref[:, cols], gains_ref[1:2, :])
        prob_low = softmax(q_norm, k_norm).astype(jnp.bfloat16)
        attn_ref[:, cols] = product(prob_low, v_ref[:, cols], 1, 0).astype(jnp.bfloat16)


def forward(queries_raw, keys_raw, values, norm_gains):
    tokens, width = queries_raw.shape
    block = pl.BlockSpec((PATCH, width), lambda i: (i, 0))
    return pl.pallas_call(
        forward_kernel,
        grid=(tokens // PATCH,),
        in_specs=[block, block, block, pl.BlockSpec((2, HD), lambda i: (0, 0))],
        out_specs=block,
        out_shape=jax.ShapeDtypeStruct((tokens, width), jnp.bfloat16),
        compiler_params=pltpu.CompilerParams(vmem_limit_bytes=VMEM_LIMIT),
    )(queries_raw, keys_raw, values, norm_gains)


def backward_kernel(
    stays_ref, q_ref, k_ref, v_ref, own_ref, p1_ref, p2_ref, p3_ref, gains_ref,
    qg_ref, kg_ref, vg_ref, terms_ref,
):
    @pl.when(pl.program_id(0) == 0)
    def _():
        terms_ref[...] = jnp.zeros_like(terms_ref)

    q_gain, k_gain = gains_ref[0:1, :], gains_ref[1:2, :]
    for head in range(q_ref.shape[1] // HD):
        cols = slice(head * HD, (head + 1) * HD)
        value = v_ref[:, cols]
        q_unit, q_inverse, q_norm = normalize(q_ref[:, cols], q_gain)
        k_unit, k_inverse, k_norm = normalize(k_ref[:, cols], k_gain)
        prob = softmax(q_norm, k_norm)
        prob_low = prob.astype(jnp.bfloat16)
        attn = product(prob_low, value, 1, 0).astype(jnp.bfloat16)
        grad = sum(ref[:, cols].astype(jnp.float32) for ref in (p1_ref, p2_ref, p3_ref))
        own = jnp.where(stays_ref[0] == 1, own_ref[:, cols].astype(jnp.float32), 0.0)
        grad = (grad + own).astype(jnp.bfloat16)
        vg_ref[:, cols] = product(prob_low, grad, 0, 0).astype(jnp.bfloat16)
        delta = jnp.sum(
            grad.astype(jnp.float32) * attn.astype(jnp.float32), axis=-1, keepdims=True
        )
        score_grad = (prob * (product(grad, value, 1, 1) - delta)).astype(jnp.bfloat16)
        qn_grad = product(score_grad, k_norm, 1, 0) * SCALE
        kn_grad = product(score_grad, q_norm, 0, 0) * SCALE
        terms_ref[0:1, :] += jnp.sum(qn_grad * q_unit, axis=0, keepdims=True)
        terms_ref[1:2, :] += jnp.sum(kn_grad * k_unit, axis=0, keepdims=True)
        qg_ref[:, cols] = unnormalize(qn_grad, q_unit, q_inverse, q_gain).astype(jnp.bfloat16)
        kg_ref[:, cols] = unnormalize(kn_grad, k_unit, k_inverse, k_gain).astype(jnp.bfloat16)


def backward(stays, queries_raw, keys_raw, values, parts, norm_gains):
    tokens, width = queries_raw.shape
    block = pl.BlockSpec((PATCH, width), lambda i, stays: (i, 0))
    gains = pl.BlockSpec((2, HD), lambda i, stays: (0, 0))
    out = jax.ShapeDtypeStruct((tokens, width), jnp.bfloat16)
    return pl.pallas_call(
        backward_kernel,
        grid_spec=pltpu.PrefetchScalarGridSpec(
            num_scalar_prefetch=1,
            grid=(tokens // PATCH,),
            in_specs=[block] * 7 + [gains],
            out_specs=[block, block, block, gains],
        ),
        out_shape=[out, out, out, jax.ShapeDtypeStruct((2, HD), jnp.float32)],
        compiler_params=pltpu.CompilerParams(vmem_limit_bytes=VMEM_LIMIT),
    )(stays, queries_raw, keys_raw, values, *parts, norm_gains)


STEPS = (0, 3, 1, 2)
CHUNK = 256


def row_block(place_ref, index):
    x = lax.rem(place_ref[0] + STEPS[index % 4], 4)
    core = place_ref[1] if index < 4 else 1 - place_ref[1]
    return 2 * x + core


def rows_of(place_ref, index, width):
    return pl.ds(pl.multiple_of(row_block(place_ref, index) * width, width), width)


def add_blocks(place_ref, attn_ref, refs, total, start):
    width = refs[0].shape[1]
    attn = attn_ref[...]
    for index in range(8):
        rows = rows_of(place_ref, index, width)
        term = product(refs[index][...], attn, 0, 0)

        @pl.when(start)
        def _():
            total[rows] = term

        @pl.when(jnp.logical_not(start))
        def _():
            total[rows] += term


def first_kernel(place_ref, attn_ref, *refs):
    add_blocks(place_ref, attn_ref, refs[:8], refs[8], pl.program_id(0) == 0)


def second_kernel(place_ref, attn_ref, *refs):
    first_ref, wgrad_ref, total = refs[8:]
    add_blocks(place_ref, attn_ref, refs[:8], total, pl.program_id(0) == 0)

    @pl.when(pl.program_id(0) == pl.num_programs(0) - 1)
    def _():
        wgrad_ref[...] = (total[...] + first_ref[...]).astype(wgrad_ref.dtype)


def weight_product(place, attn, blocks, first=None):
    tokens, width = blocks[0].shape
    heads = attn.shape[1]
    rows = 8 * width
    whole = pl.BlockSpec((rows, heads), lambda i, place: (0, 0))
    last = first is not None
    return pl.pallas_call(
        second_kernel if last else first_kernel,
        grid_spec=pltpu.PrefetchScalarGridSpec(
            num_scalar_prefetch=1,
            grid=(tokens // CHUNK,),
            in_specs=[pl.BlockSpec((CHUNK, heads), lambda i, place: (i, 0))]
            + [pl.BlockSpec((CHUNK, width), lambda i, place: (i, 0))] * 8
            + [whole] * last,
            out_specs=whole,
            scratch_shapes=[pltpu.VMEM((rows, heads), jnp.float32)] * last,
        ),
        out_shape=jax.ShapeDtypeStruct((rows, heads), jnp.bfloat16 if last else jnp.float32),
        compiler_params=pltpu.CompilerParams(vmem_limit_bytes=VMEM_LIMIT),
        cost_estimate=pl.CostEstimate(
            flops=2 * rows * tokens * heads,
            bytes_accessed=2 * rows * (tokens + 2 * heads),
            transcendentals=0,
        ),
    )(place, attn, *blocks, *([first] if last else []))


def token_kernel(place_ref, weight_ref, *refs):
    blocks, part_ref = refs[:8], refs[8]
    width = blocks[0].shape[1]
    total = None
    for index in range(8):
        term = product(blocks[index][...], weight_ref[rows_of(place_ref, index, width)], 1, 0)
        total = term if total is None else total + term
    part_ref[...] = total.astype(part_ref.dtype)


def token_product(place, blocks, weights):
    tokens, width = blocks[0].shape
    rows, heads = weights.shape
    return pl.pallas_call(
        token_kernel,
        grid_spec=pltpu.PrefetchScalarGridSpec(
            num_scalar_prefetch=1,
            grid=(tokens // CHUNK,),
            in_specs=[pl.BlockSpec((rows, heads), lambda i, place: (0, 0))]
            + [pl.BlockSpec((CHUNK, width), lambda i, place: (i, 0))] * 8,
            out_specs=pl.BlockSpec((CHUNK, heads), lambda i, place: (i, 0)),
        ),
        out_shape=jax.ShapeDtypeStruct((tokens, heads), jnp.bfloat16),
        compiler_params=pltpu.CompilerParams(vmem_limit_bytes=VMEM_LIMIT),
        cost_estimate=pl.CostEstimate(
            flops=2 * rows * tokens * heads,
            bytes_accessed=2 * rows * (tokens + heads),
            transcendentals=0,
        ),
    )(place, weights, *blocks)


def swap_y(array, target):
    pairs = []
    for low in range(2):
        for high in range(2):
            place = target(low, high)
            if place is not None:
                pairs.append((low * 2 + high, place[0] * 2 + place[1]))
    return lax.ppermute(array, ("yl", "yh"), pairs)


def to_partner(array):
    return lax.ppermute(array, "yl", [(0, 1), (1, 0)])


def to_core(array):
    return lax.ppermute(array, "c", [(0, 1), (1, 0)])


def along_x(array, step):
    return lax.ppermute(array, "x", [(x, (x + step) % 4) for x in range(4)])


def round_x(block):
    blocks = [block, along_x(block, 1), along_x(block, -1), along_x(block, 2)]
    return blocks + [to_core(piece) for piece in blocks]


def sum_over(array, axis, count):
    spread = lax.all_to_all(jnp.broadcast_to(array[None], (count,) + array.shape), axis, 0, 0)
    return jnp.sum(spread, axis=0)


def per_device(queries_raw, keys_raw, values, grad_out, out_weight, norm_gains):
    place = jnp.stack([lax.axis_index("x"), lax.axis_index("c")]).astype(jnp.int32)
    stays = lax.axis_index("yl") == lax.axis_index("yh")
    turn = lambda low, up: (up, low)
    weights = lax.all_gather(swap_y(out_weight, turn), "z", axis=0, tiled=True)
    own = round_x(grad_out)
    other = round_x(to_partner(grad_out))

    attn = forward(queries_raw, keys_raw, values, norm_gains)
    turned = swap_y(attn, turn)
    crossed = swap_y(attn, lambda low, up: (up, 1 - low))
    own_attn = jnp.where(stays, turned, crossed)
    other_attn = jnp.where(stays, crossed, turned)
    first = weight_product(place, own_attn, own)
    wgrad = weight_product(place, other_attn, other, first)
    shard = lax.psum_scatter(wgrad, "z", scatter_dimension=0, tiled=True)

    weights, _ = lax.optimization_barrier((weights, wgrad))
    part_other = token_product(place, other, weights)
    weights, _ = lax.optimization_barrier((weights, part_other))
    part_own = token_product(place, own, weights)
    parts = [
        part_own,
        swap_y(part_other, lambda low, up: (1 - low, low) if low == up else None),
        swap_y(part_other, lambda low, up: (1 - low, low) if low != up else None),
        swap_y(part_own, lambda low, up: (low, low) if low != up else None),
    ]
    queries_grad, keys_grad, values_grad, terms = backward(
        stays.astype(jnp.int32).reshape(1), queries_raw, keys_raw, values, parts, norm_gains
    )
    gains_grad = sum_over(sum_over(terms, ("yl", "yh", "x", "c"), 32), "z", 16)
    shard, gains_grad = lax.optimization_barrier((shard, gains_grad))
    weight_grad = swap_y(shard, turn).astype(jnp.float32)
    return (queries_grad, keys_grad, values_grad, weight_grad, gains_grad)


def solution(mesh):
    fine = Mesh(mesh.devices.reshape(SIZES), AXES)
    spec = P(("yl", "z"), ("yh", "x", "c"))
    return jax.shard_map(
        per_device,
        mesh=fine,
        in_specs=(spec, spec, spec, spec, spec, P()),
        out_specs=(spec, spec, spec, spec, P()),
        check_vma=False,
    )
```

```python
import jax
import jax.numpy as jnp
from jax import lax
from jax.experimental import pallas as pl
from jax.experimental.pallas import tpu as pltpu
from jax.sharding import Mesh, PartitionSpec as P

HD = 128
PATCH = 256
EPSILON = 1e-06
SCALE = HD ** (-0.5)
AXES = ("yl", "za", "zm", "zl", "yh", "x", "c")
SIZES = (2, 4, 2, 2, 2, 4, 2)
Z = ("za", "zm", "zl")
VMEM_LIMIT = 56 * 1024 * 1024


def normalize(raw, gain):
    values32 = raw.astype(jnp.float32)
    center = values32 - jnp.mean(values32, axis=-1, keepdims=True)
    inverse = lax.rsqrt(jnp.mean(center * center, axis=-1, keepdims=True) + EPSILON)
    unit = center * inverse
    return (unit, inverse, (unit * gain).astype(jnp.bfloat16))


def unnormalize(grad, unit, inverse, gain):
    scaled = grad * gain
    centered = scaled - jnp.mean(scaled, axis=-1, keepdims=True)
    return (centered - unit * jnp.mean(scaled * unit, axis=-1, keepdims=True)) * inverse


def product(left, right, left_dim, right_dim):
    return lax.dot_general(
        left, right, (((left_dim,), (right_dim,)), ((), ())), preferred_element_type=jnp.float32
    )


def softmax(q_norm, k_norm):
    scores = product(q_norm, k_norm, 1, 1) * SCALE
    expo = jnp.exp(scores - jnp.max(scores, axis=-1, keepdims=True))
    return expo / jnp.sum(expo, axis=-1, keepdims=True)


def forward_kernel(q_ref, k_ref, v_ref, gains_ref, attn_ref):
    for head in range(q_ref.shape[1] // HD):
        cols = slice(head * HD, (head + 1) * HD)
        _, _, q_norm = normalize(q_ref[:, cols], gains_ref[0:1, :])
        _, _, k_norm = normalize(k_ref[:, cols], gains_ref[1:2, :])
        prob_low = softmax(q_norm, k_norm).astype(jnp.bfloat16)
        attn_ref[:, cols] = product(prob_low, v_ref[:, cols], 1, 0).astype(jnp.bfloat16)


def forward(queries_raw, keys_raw, values, norm_gains):
    tokens, width = queries_raw.shape
    block = pl.BlockSpec((PATCH, width), lambda i: (i, 0))
    return pl.pallas_call(
        forward_kernel,
        grid=(tokens // PATCH,),
        in_specs=[block, block, block, pl.BlockSpec((2, HD), lambda i: (0, 0))],
        out_specs=block,
        out_shape=jax.ShapeDtypeStruct((tokens, width), jnp.bfloat16),
        compiler_params=pltpu.CompilerParams(vmem_limit_bytes=VMEM_LIMIT),
    )(queries_raw, keys_raw, values, norm_gains)


def backward_kernel(
    q_ref, k_ref, v_ref, one_ref, two_ref, gains_ref, qg_ref, kg_ref, vg_ref, terms_ref
):
    @pl.when(pl.program_id(0) == 0)
    def _():
        terms_ref[...] = jnp.zeros_like(terms_ref)

    q_gain, k_gain = gains_ref[0:1, :], gains_ref[1:2, :]
    for head in range(q_ref.shape[1] // HD):
        cols = slice(head * HD, (head + 1) * HD)
        value = v_ref[:, cols]
        q_unit, q_inverse, q_norm = normalize(q_ref[:, cols], q_gain)
        k_unit, k_inverse, k_norm = normalize(k_ref[:, cols], k_gain)
        prob = softmax(q_norm, k_norm)
        prob_low = prob.astype(jnp.bfloat16)
        attn = product(prob_low, value, 1, 0).astype(jnp.bfloat16)
        grad = one_ref[:, cols].astype(jnp.float32) + two_ref[:, cols].astype(jnp.float32)
        grad = grad.astype(jnp.bfloat16)
        vg_ref[:, cols] = product(prob_low, grad, 0, 0).astype(jnp.bfloat16)
        delta = jnp.sum(
            grad.astype(jnp.float32) * attn.astype(jnp.float32), axis=-1, keepdims=True
        )
        score_grad = (prob * (product(grad, value, 1, 1) - delta)).astype(jnp.bfloat16)
        qn_grad = product(score_grad, k_norm, 1, 0) * SCALE
        kn_grad = product(score_grad, q_norm, 0, 0) * SCALE
        terms_ref[0:1, :] += jnp.sum(qn_grad * q_unit, axis=0, keepdims=True)
        terms_ref[1:2, :] += jnp.sum(kn_grad * k_unit, axis=0, keepdims=True)
        qg_ref[:, cols] = unnormalize(qn_grad, q_unit, q_inverse, q_gain).astype(jnp.bfloat16)
        kg_ref[:, cols] = unnormalize(kn_grad, k_unit, k_inverse, k_gain).astype(jnp.bfloat16)


def backward(queries_raw, keys_raw, values, part_one, part_two, norm_gains):
    tokens, width = queries_raw.shape
    block = pl.BlockSpec((PATCH, width), lambda i: (i, 0))
    gains = pl.BlockSpec((2, HD), lambda i: (0, 0))
    out = jax.ShapeDtypeStruct((tokens, width), jnp.bfloat16)
    return pl.pallas_call(
        backward_kernel,
        grid=(tokens // PATCH,),
        in_specs=[block] * 5 + [gains],
        out_specs=[block, block, block, gains],
        out_shape=[out, out, out, jax.ShapeDtypeStruct((2, HD), jnp.float32)],
        compiler_params=pltpu.CompilerParams(vmem_limit_bytes=VMEM_LIMIT),
    )(queries_raw, keys_raw, values, part_one, part_two, norm_gains)


def weight_kernel(place_ref, grad_ref, same_ref, other_ref, keep_ref, give_ref):
    high, parity = place_ref[0], place_ref[1]
    rows = keep_ref.shape[1]
    for core in range(2):
        term = product(grad_ref[high, 0, core], same_ref[...], 0, 0)
        term += product(grad_ref[1 - high, 0, core], other_ref[...], 0, 0)
        term = term.astype(keep_ref.dtype)
        even, odd = term[:rows], term[rows:]
        keep_ref[core] = jnp.where(parity == 0, even, odd)
        give_ref[core] = jnp.where(parity == 0, odd, even)


def weight_product(place, grads, attn_same, attn_other):
    _, blocks, cores, tokens, width = grads.shape
    heads = attn_same.shape[1]
    attn = pl.BlockSpec((tokens, heads), lambda x, place: (0, 0))
    slab = pl.BlockSpec((cores, width // 2, heads), lambda x, place: (x, 0, 0))
    out = jax.ShapeDtypeStruct((blocks * cores, width // 2, heads), jnp.bfloat16)
    return pl.pallas_call(
        weight_kernel,
        grid_spec=pltpu.PrefetchScalarGridSpec(
            num_scalar_prefetch=1,
            grid=(blocks,),
            in_specs=[
                pl.BlockSpec((2, 1) + grads.shape[2:], lambda x, place: (0, x, 0, 0, 0)),
                attn,
                attn,
            ],
            out_specs=[slab, slab],
        ),
        out_shape=[out, out],
        compiler_params=pltpu.CompilerParams(vmem_limit_bytes=VMEM_LIMIT),
        cost_estimate=pl.CostEstimate(
            flops=2 * grads.size * heads,
            bytes_accessed=2 * (grads.size + blocks * cores * width * heads),
            transcendentals=0,
        ),
    )(place, grads, attn_same, attn_other)


def token_kernel(low_ref, grad_ref, weight_ref, part_ref, total):
    step = pl.program_id(0)
    weights = weight_ref[...].reshape(-1, weight_ref.shape[3])
    width = grad_ref.shape[4]
    term = product(grad_ref[0, 0, 0], weights[:width], 1, 0)
    term += product(grad_ref[0, 0, 1], weights[width:], 1, 0)

    @pl.when(step == 0)
    def _():
        total[...] = term

    @pl.when(step > 0)
    def _():
        total[...] += term

    @pl.when(step == pl.num_programs(0) - 1)
    def _():
        part_ref[...] = total[...].astype(part_ref.dtype)


def token_product(low, grads, weights):
    _, blocks, _, tokens, _ = grads.shape
    fours, _, rows, heads = weights.shape
    return pl.pallas_call(
        token_kernel,
        grid_spec=pltpu.PrefetchScalarGridSpec(
            num_scalar_prefetch=1,
            grid=(blocks,),
            in_specs=[
                pl.BlockSpec((1, 1) + grads.shape[2:], lambda x, low: (low[0], x, 0, 0, 0)),
                pl.BlockSpec((fours, 1, rows, heads), lambda x, low: (0, x, 0, 0)),
            ],
            out_specs=pl.BlockSpec((tokens, heads), lambda x, low: (0, 0)),
            scratch_shapes=[pltpu.VMEM((tokens, heads), jnp.float32)],
        ),
        out_shape=jax.ShapeDtypeStruct((tokens, heads), jnp.bfloat16),
        compiler_params=pltpu.CompilerParams(vmem_limit_bytes=VMEM_LIMIT),
        cost_estimate=pl.CostEstimate(
            flops=grads.size * heads,
            bytes_accessed=grads.size + 2 * weights.size,
            transcendentals=0,
        ),
    )(low, grads, weights)


def swap_y(array, target):
    pairs = []
    for low in range(2):
        for high in range(2):
            to_low, to_high = target(low, high)
            pairs.append((low * 2 + high, to_low * 2 + to_high))
    return lax.ppermute(array, ("yl", "yh"), pairs)


def turned(array):
    return swap_y(array, lambda low, high: (high, low))


def along(array, step):
    return lax.ppermute(array, Z, [(z, (z + step) % 16) for z in range(16)])


def gather_rows(own_rows):
    column = lax.all_gather(own_rows, "za", axis=0)
    before = along(column, 1)
    after = along(column, -1)
    far = jnp.concatenate([along(column[:2], 2), along(column[2:], -2)])
    blocks = [column, after, far, before]
    shift = (4 - lax.axis_index(("zm", "zl"))) % 4
    return lax.dynamic_slice_in_dim(jnp.stack(blocks + blocks), shift, 4, axis=0)


def pair_terms(give):
    half = give.shape[0] // 2
    return along(give[:half], 1), along(give[half:], -1)


def sum_over(array, axis, count):
    spread = lax.all_to_all(jnp.broadcast_to(array[None], (count,) + array.shape), axis, 0, 0)
    return jnp.sum(spread, axis=0)


def per_device(queries_raw, keys_raw, values, grad_out, out_weight, norm_gains):
    high = lax.axis_index("yh").astype(jnp.int32).reshape(1)
    place = jnp.concatenate([high, lax.axis_index("zl").astype(jnp.int32).reshape(1)])
    grads = lax.all_gather(grad_out, ("yl", "x", "c"), axis=0)
    grads = grads.reshape((2, 4, 2) + grad_out.shape)

    attn = forward(queries_raw, keys_raw, values, norm_gains)
    attn_same = turned(attn)
    attn_other = swap_y(attn, lambda low, up: (up, 1 - low))
    weights = gather_rows(turned(out_weight))
    grads, weights = lax.optimization_barrier((grads, weights))

    keep, give = weight_product(place, grads, attn_same, attn_other)
    before, after = pair_terms(give)
    weights, _ = lax.optimization_barrier((weights, give))
    part_other = token_product(1 - high, grads, weights)

    before, after, part_other = lax.optimization_barrier((before, after, part_other))
    came = jnp.concatenate([before, after]).astype(jnp.float32)
    column = (keep.astype(jnp.float32) + came).astype(keep.dtype)
    shard = lax.psum_scatter(column, ("za", "zm"), scatter_dimension=0)

    weights, _ = lax.optimization_barrier((weights, column))
    part_same = token_product(high, grads, weights)
    came_other = swap_y(part_other, lambda low, up: (1 - up, low))
    came_same = turned(part_same)
    queries_grad, keys_grad, values_grad, terms = backward(
        queries_raw, keys_raw, values, came_same, came_other, norm_gains
    )
    gains_grad = sum_over(sum_over(terms, ("yl", "yh", "x", "c"), 32), Z, 16)
    shard, gains_grad = lax.optimization_barrier((shard, gains_grad))
    weight_grad = turned(shard).astype(jnp.float32)
    return (queries_grad, keys_grad, values_grad, weight_grad, gains_grad)


def solution(mesh):
    fine = Mesh(mesh.devices.reshape(SIZES), AXES)
    spec = P(("yl", "za", "zm", "zl"), ("yh", "x", "c"))
    return jax.shard_map(
        per_device,
        mesh=fine,
        in_specs=(spec, spec, spec, spec, spec, P()),
        out_specs=(spec, spec, spec, spec, P()),
        check_vma=False,
    )
```

```python
import jax
import jax.numpy as jnp
from jax import lax
from jax.experimental import pallas as pl
from jax.experimental.pallas import tpu as pltpu
from jax.sharding import Mesh, PartitionSpec as P

HD = 128
PATCH = 256
EPSILON = 1e-06
SCALE = HD ** (-0.5)
AXES = ("yl", "za", "zb", "yh", "x", "c")
SIZES = (2, 4, 4, 2, 4, 2)
Z = ("za", "zb")
VMEM_LIMIT = 56 * 1024 * 1024


def normalize(raw, gain):
    values32 = raw.astype(jnp.float32)
    center = values32 - jnp.mean(values32, axis=-1, keepdims=True)
    inverse = lax.rsqrt(jnp.mean(center * center, axis=-1, keepdims=True) + EPSILON)
    unit = center * inverse
    return (unit, inverse, (unit * gain).astype(jnp.bfloat16))


def unnormalize(grad, unit, inverse, gain):
    scaled = grad * gain
    centered = scaled - jnp.mean(scaled, axis=-1, keepdims=True)
    return (centered - unit * jnp.mean(scaled * unit, axis=-1, keepdims=True)) * inverse


def product(left, right, left_dim, right_dim):
    return lax.dot_general(
        left, right, (((left_dim,), (right_dim,)), ((), ())), preferred_element_type=jnp.float32
    )


def softmax(q_norm, k_norm):
    scores = product(q_norm, k_norm, 1, 1) * SCALE
    expo = jnp.exp(scores - jnp.max(scores, axis=-1, keepdims=True))
    return expo / jnp.sum(expo, axis=-1, keepdims=True)


def forward_kernel(q_ref, k_ref, v_ref, gains_ref, attn_ref):
    for head in range(q_ref.shape[1] // HD):
        cols = slice(head * HD, (head + 1) * HD)
        _, _, q_norm = normalize(q_ref[:, cols], gains_ref[0:1, :])
        _, _, k_norm = normalize(k_ref[:, cols], gains_ref[1:2, :])
        prob_low = softmax(q_norm, k_norm).astype(jnp.bfloat16)
        attn_ref[:, cols] = product(prob_low, v_ref[:, cols], 1, 0).astype(jnp.bfloat16)


def forward(queries_raw, keys_raw, values, norm_gains):
    tokens, width = queries_raw.shape
    block = pl.BlockSpec((PATCH, width), lambda i: (i, 0))
    return pl.pallas_call(
        forward_kernel,
        grid=(tokens // PATCH,),
        in_specs=[block, block, block, pl.BlockSpec((2, HD), lambda i: (0, 0))],
        out_specs=block,
        out_shape=jax.ShapeDtypeStruct((tokens, width), jnp.bfloat16),
        compiler_params=pltpu.CompilerParams(vmem_limit_bytes=VMEM_LIMIT),
    )(queries_raw, keys_raw, values, norm_gains)


def backward_kernel(
    q_ref, k_ref, v_ref, one_ref, two_ref, gains_ref, qg_ref, kg_ref, vg_ref, terms_ref
):
    @pl.when(pl.program_id(0) == 0)
    def _():
        terms_ref[...] = jnp.zeros_like(terms_ref)

    q_gain, k_gain = gains_ref[0:1, :], gains_ref[1:2, :]
    for head in range(q_ref.shape[1] // HD):
        cols = slice(head * HD, (head + 1) * HD)
        value = v_ref[:, cols]
        q_unit, q_inverse, q_norm = normalize(q_ref[:, cols], q_gain)
        k_unit, k_inverse, k_norm = normalize(k_ref[:, cols], k_gain)
        prob = softmax(q_norm, k_norm)
        prob_low = prob.astype(jnp.bfloat16)
        attn = product(prob_low, value, 1, 0).astype(jnp.bfloat16)
        grad = one_ref[:, cols].astype(jnp.float32) + two_ref[:, cols].astype(jnp.float32)
        grad = grad.astype(jnp.bfloat16)
        vg_ref[:, cols] = product(prob_low, grad, 0, 0).astype(jnp.bfloat16)
        delta = jnp.sum(
            grad.astype(jnp.float32) * attn.astype(jnp.float32), axis=-1, keepdims=True
        )
        score_grad = (prob * (product(grad, value, 1, 1) - delta)).astype(jnp.bfloat16)
        qn_grad = product(score_grad, k_norm, 1, 0) * SCALE
        kn_grad = product(score_grad, q_norm, 0, 0) * SCALE
        terms_ref[0:1, :] += jnp.sum(qn_grad * q_unit, axis=0, keepdims=True)
        terms_ref[1:2, :] += jnp.sum(kn_grad * k_unit, axis=0, keepdims=True)
        qg_ref[:, cols] = unnormalize(qn_grad, q_unit, q_inverse, q_gain).astype(jnp.bfloat16)
        kg_ref[:, cols] = unnormalize(kn_grad, k_unit, k_inverse, k_gain).astype(jnp.bfloat16)


def backward(queries_raw, keys_raw, values, part_one, part_two, norm_gains):
    tokens, width = queries_raw.shape
    block = pl.BlockSpec((PATCH, width), lambda i: (i, 0))
    gains = pl.BlockSpec((2, HD), lambda i: (0, 0))
    out = jax.ShapeDtypeStruct((tokens, width), jnp.bfloat16)
    return pl.pallas_call(
        backward_kernel,
        grid=(tokens // PATCH,),
        in_specs=[block] * 5 + [gains],
        out_specs=[block, block, block, gains],
        out_shape=[out, out, out, jax.ShapeDtypeStruct((2, HD), jnp.float32)],
        compiler_params=pltpu.CompilerParams(vmem_limit_bytes=VMEM_LIMIT),
    )(queries_raw, keys_raw, values, part_one, part_two, norm_gains)


def weight_kernel(high_ref, grad_ref, same_ref, other_ref, wgrad_ref):
    high = high_ref[0]
    width = grad_ref.shape[4]
    for core in range(2):
        term = product(grad_ref[high, 0, core], same_ref[...], 0, 0)
        term += product(grad_ref[1 - high, 0, core], other_ref[...], 0, 0)
        wgrad_ref[core * width : (core + 1) * width] = term.astype(wgrad_ref.dtype)


def grad_block(grads):
    return pl.BlockSpec((2, 1) + grads.shape[2:], lambda x, high: (0, x, 0, 0, 0))


def weight_product(high, grads, attn_same, attn_other):
    _, blocks, cores, tokens, width = grads.shape
    heads = attn_same.shape[1]
    attn = pl.BlockSpec((tokens, heads), lambda x, high: (0, 0))
    return pl.pallas_call(
        weight_kernel,
        grid_spec=pltpu.PrefetchScalarGridSpec(
            num_scalar_prefetch=1,
            grid=(blocks,),
            in_specs=[grad_block(grads), attn, attn],
            out_specs=pl.BlockSpec((cores * width, heads), lambda x, high: (x, 0)),
        ),
        out_shape=jax.ShapeDtypeStruct((blocks * cores * width, heads), jnp.bfloat16),
        compiler_params=pltpu.CompilerParams(vmem_limit_bytes=VMEM_LIMIT),
        cost_estimate=pl.CostEstimate(
            flops=2 * grads.size * heads,
            bytes_accessed=2 * (grads.size + blocks * cores * width * heads),
            transcendentals=0,
        ),
    )(high, grads, attn_same, attn_other)


def token_kernel(high_ref, grad_ref, weight_ref, same_ref, other_ref, total):
    step = pl.program_id(0)
    high = high_ref[0]
    weights = weight_ref[...].reshape(-1, weight_ref.shape[3])
    width = grad_ref.shape[4]

    @pl.when(step == 0)
    def _():
        total[...] = jnp.zeros_like(total)

    for index, low in enumerate((high, 1 - high)):
        term = product(grad_ref[low, 0, 0], weights[:width], 1, 0)
        total[index] += term + product(grad_ref[low, 0, 1], weights[width:], 1, 0)

    @pl.when(step == pl.num_programs(0) - 1)
    def _():
        same_ref[...] = total[0].astype(same_ref.dtype)
        other_ref[...] = total[1].astype(other_ref.dtype)


def token_product(high, grads, weights):
    _, blocks, _, tokens, _ = grads.shape
    fours, _, rows, heads = weights.shape
    out = jax.ShapeDtypeStruct((tokens, heads), jnp.bfloat16)
    return pl.pallas_call(
        token_kernel,
        grid_spec=pltpu.PrefetchScalarGridSpec(
            num_scalar_prefetch=1,
            grid=(blocks,),
            in_specs=[
                grad_block(grads),
                pl.BlockSpec((fours, 1, rows, heads), lambda x, high: (0, x, 0, 0)),
            ],
            out_specs=[pl.BlockSpec((tokens, heads), lambda x, high: (0, 0))] * 2,
            scratch_shapes=[pltpu.VMEM((2, tokens, heads), jnp.float32)],
        ),
        out_shape=[out, out],
        compiler_params=pltpu.CompilerParams(vmem_limit_bytes=VMEM_LIMIT),
        cost_estimate=pl.CostEstimate(
            flops=2 * grads.size * heads,
            bytes_accessed=2 * (grads.size + weights.size),
            transcendentals=0,
        ),
    )(high, grads, weights)


def swap_y(array, target):
    pairs = []
    for low in range(2):
        for high in range(2):
            to_low, to_high = target(low, high)
            pairs.append((low * 2 + high, to_low * 2 + to_high))
    return lax.ppermute(array, ("yl", "yh"), pairs)


def turned(array):
    return swap_y(array, lambda low, high: (high, low))


def along(array, step):
    return lax.ppermute(array, Z, [(z, (z + step) % 16) for z in range(16)])


def gather_rows(own_rows):
    column = lax.all_gather(own_rows, "za", axis=0)
    before = along(column, 1)
    after = along(column, -1)
    far = jnp.concatenate([along(column[:2], 2), along(column[2:], -2)])
    blocks = [column, after, far, before]
    shift = (4 - lax.axis_index("zb")) % 4
    return lax.dynamic_slice_in_dim(jnp.stack(blocks + blocks), shift, 4, axis=0)


def sum_over(array, axis, count):
    spread = lax.all_to_all(jnp.broadcast_to(array[None], (count,) + array.shape), axis, 0, 0)
    return jnp.sum(spread, axis=0)


def per_device(queries_raw, keys_raw, values, grad_out, out_weight, norm_gains):
    high = lax.axis_index("yh").reshape(1)
    grads = lax.all_gather(grad_out, ("yl", "x", "c"), axis=0)
    grads = grads.reshape((2, 4, 2) + grad_out.shape)

    attn = forward(queries_raw, keys_raw, values, norm_gains)
    attn_same = turned(attn)
    attn_other = swap_y(attn, lambda low, up: (up, 1 - low))
    own_rows, _ = lax.optimization_barrier((turned(out_weight), attn))
    weights = gather_rows(own_rows)
    grads, weights = lax.optimization_barrier((grads, weights))

    wgrad = weight_product(high, grads, attn_same, attn_other)
    shard = lax.psum_scatter(wgrad, Z, scatter_dimension=0, tiled=True)

    weights, _ = lax.optimization_barrier((weights, wgrad))
    part_same, part_other = token_product(high, grads, weights)
    came_same = turned(part_same)
    came_other = swap_y(part_other, lambda low, up: (1 - up, low))
    queries_grad, keys_grad, values_grad, terms = backward(
        queries_raw, keys_raw, values, came_same, came_other, norm_gains
    )
    gains_grad = sum_over(sum_over(terms, ("yl", "yh", "x", "c"), 32), Z, 16)
    shard, gains_grad = lax.optimization_barrier((shard, gains_grad))
    weight_grad = turned(shard).astype(jnp.float32)
    return (queries_grad, keys_grad, values_grad, weight_grad, gains_grad)


def solution(mesh):
    fine = Mesh(mesh.devices.reshape(SIZES), AXES)
    spec = P(("yl", "za", "zb"), ("yh", "x", "c"))
    return jax.shard_map(
        per_device,
        mesh=fine,
        in_specs=(spec, spec, spec, spec, spec, P()),
        out_specs=(spec, spec, spec, spec, P()),
        check_vma=False,
    )
```

```python
import jax
import jax.numpy as jnp
from jax import lax
from jax.experimental import pallas as pl
from jax.experimental.pallas import tpu as pltpu
from jax.sharding import Mesh, PartitionSpec as P

HD = 128
PATCH = 256
EPSILON = 1e-06
SCALE = HD ** (-0.5)
AXES = ("yl", "za", "zb", "yh", "x", "c")
SIZES = (2, 4, 4, 2, 4, 2)
Z = ("za", "zb")
VMEM_LIMIT = 56 * 1024 * 1024


def normalize(raw, gain):
    values32 = raw.astype(jnp.float32)
    center = values32 - jnp.mean(values32, axis=-1, keepdims=True)
    inverse = lax.rsqrt(jnp.mean(center * center, axis=-1, keepdims=True) + EPSILON)
    unit = center * inverse
    return (unit, inverse, (unit * gain).astype(jnp.bfloat16))


def unnormalize(grad, unit, inverse, gain):
    scaled = grad * gain
    centered = scaled - jnp.mean(scaled, axis=-1, keepdims=True)
    return (centered - unit * jnp.mean(scaled * unit, axis=-1, keepdims=True)) * inverse


def product(left, right, left_dim, right_dim):
    return lax.dot_general(
        left, right, (((left_dim,), (right_dim,)), ((), ())), preferred_element_type=jnp.float32
    )


def softmax(q_norm, k_norm):
    scores = product(q_norm, k_norm, 1, 1) * SCALE
    expo = jnp.exp(scores - jnp.max(scores, axis=-1, keepdims=True))
    return expo / jnp.sum(expo, axis=-1, keepdims=True)


def forward_kernel(q_ref, k_ref, v_ref, gains_ref, attn_ref):
    for head in range(q_ref.shape[1] // HD):
        cols = slice(head * HD, (head + 1) * HD)
        _, _, q_norm = normalize(q_ref[:, cols], gains_ref[0:1, :])
        _, _, k_norm = normalize(k_ref[:, cols], gains_ref[1:2, :])
        prob_low = softmax(q_norm, k_norm).astype(jnp.bfloat16)
        attn_ref[:, cols] = product(prob_low, v_ref[:, cols], 1, 0).astype(jnp.bfloat16)


def forward(queries_raw, keys_raw, values, norm_gains):
    tokens, width = queries_raw.shape
    block = pl.BlockSpec((PATCH, width), lambda i: (i, 0))
    return pl.pallas_call(
        forward_kernel,
        grid=(tokens // PATCH,),
        in_specs=[block, block, block, pl.BlockSpec((2, HD), lambda i: (0, 0))],
        out_specs=block,
        out_shape=jax.ShapeDtypeStruct((tokens, width), jnp.bfloat16),
        compiler_params=pltpu.CompilerParams(vmem_limit_bytes=VMEM_LIMIT),
    )(queries_raw, keys_raw, values, norm_gains)


def backward_kernel(
    q_ref, k_ref, v_ref, one_ref, two_ref, gains_ref, qg_ref, kg_ref, vg_ref, terms_ref
):
    @pl.when(pl.program_id(0) == 0)
    def _():
        terms_ref[...] = jnp.zeros_like(terms_ref)

    q_gain, k_gain = gains_ref[0:1, :], gains_ref[1:2, :]
    for head in range(q_ref.shape[1] // HD):
        cols = slice(head * HD, (head + 1) * HD)
        value = v_ref[:, cols]
        q_unit, q_inverse, q_norm = normalize(q_ref[:, cols], q_gain)
        k_unit, k_inverse, k_norm = normalize(k_ref[:, cols], k_gain)
        prob = softmax(q_norm, k_norm)
        prob_low = prob.astype(jnp.bfloat16)
        attn = product(prob_low, value, 1, 0).astype(jnp.bfloat16)
        grad = one_ref[:, cols].astype(jnp.float32) + two_ref[:, cols].astype(jnp.float32)
        grad = grad.astype(jnp.bfloat16)
        vg_ref[:, cols] = product(prob_low, grad, 0, 0).astype(jnp.bfloat16)
        delta = jnp.sum(
            grad.astype(jnp.float32) * attn.astype(jnp.float32), axis=-1, keepdims=True
        )
        score_grad = (prob * (product(grad, value, 1, 1) - delta)).astype(jnp.bfloat16)
        qn_grad = product(score_grad, k_norm, 1, 0) * SCALE
        kn_grad = product(score_grad, q_norm, 0, 0) * SCALE
        terms_ref[0:1, :] += jnp.sum(qn_grad * q_unit, axis=0, keepdims=True)
        terms_ref[1:2, :] += jnp.sum(kn_grad * k_unit, axis=0, keepdims=True)
        qg_ref[:, cols] = unnormalize(qn_grad, q_unit, q_inverse, q_gain).astype(jnp.bfloat16)
        kg_ref[:, cols] = unnormalize(kn_grad, k_unit, k_inverse, k_gain).astype(jnp.bfloat16)


def backward(queries_raw, keys_raw, values, part_one, part_two, norm_gains):
    tokens, width = queries_raw.shape
    block = pl.BlockSpec((PATCH, width), lambda i: (i, 0))
    gains = pl.BlockSpec((2, HD), lambda i: (0, 0))
    out = jax.ShapeDtypeStruct((tokens, width), jnp.bfloat16)
    return pl.pallas_call(
        backward_kernel,
        grid=(tokens // PATCH,),
        in_specs=[block] * 5 + [gains],
        out_specs=[block, block, block, gains],
        out_shape=[out, out, out, jax.ShapeDtypeStruct((2, HD), jnp.float32)],
        compiler_params=pltpu.CompilerParams(vmem_limit_bytes=VMEM_LIMIT),
    )(queries_raw, keys_raw, values, part_one, part_two, norm_gains)


def weight_kernel(high_ref, grad_ref, same_ref, other_ref, wgrad_ref):
    high = high_ref[0]
    width = grad_ref.shape[4]
    for core in range(2):
        term = product(grad_ref[high, 0, core], same_ref[...], 0, 0)
        term += product(grad_ref[1 - high, 0, core], other_ref[...], 0, 0)
        wgrad_ref[core * width : (core + 1) * width] = term.astype(wgrad_ref.dtype)


def grad_block(grads):
    return pl.BlockSpec((2, 1) + grads.shape[2:], lambda x, high: (0, x, 0, 0, 0))


def weight_product(high, grads, attn_same, attn_other):
    _, blocks, cores, tokens, width = grads.shape
    heads = attn_same.shape[1]
    attn = pl.BlockSpec((tokens, heads), lambda x, high: (0, 0))
    return pl.pallas_call(
        weight_kernel,
        grid_spec=pltpu.PrefetchScalarGridSpec(
            num_scalar_prefetch=1,
            grid=(blocks,),
            in_specs=[grad_block(grads), attn, attn],
            out_specs=pl.BlockSpec((cores * width, heads), lambda x, high: (x, 0)),
        ),
        out_shape=jax.ShapeDtypeStruct((blocks * cores * width, heads), jnp.bfloat16),
        compiler_params=pltpu.CompilerParams(vmem_limit_bytes=VMEM_LIMIT),
        cost_estimate=pl.CostEstimate(
            flops=2 * grads.size * heads,
            bytes_accessed=2 * (grads.size + blocks * cores * width * heads),
            transcendentals=0,
        ),
    )(high, grads, attn_same, attn_other)


def token_kernel(high_ref, grad_ref, weight_ref, same_ref, other_ref, total):
    step = pl.program_id(0)
    high = high_ref[0]
    weights = weight_ref[...].reshape(-1, weight_ref.shape[3])
    width = grad_ref.shape[4]

    @pl.when(step == 0)
    def _():
        total[...] = jnp.zeros_like(total)

    for index, low in enumerate((high, 1 - high)):
        term = product(grad_ref[low, 0, 0], weights[:width], 1, 0)
        total[index] += term + product(grad_ref[low, 0, 1], weights[width:], 1, 0)

    @pl.when(step == pl.num_programs(0) - 1)
    def _():
        same_ref[...] = total[0].astype(same_ref.dtype)
        other_ref[...] = total[1].astype(other_ref.dtype)


def token_product(high, grads, weights):
    _, blocks, _, tokens, _ = grads.shape
    fours, _, rows, heads = weights.shape
    out = jax.ShapeDtypeStruct((tokens, heads), jnp.bfloat16)
    return pl.pallas_call(
        token_kernel,
        grid_spec=pltpu.PrefetchScalarGridSpec(
            num_scalar_prefetch=1,
            grid=(blocks,),
            in_specs=[
                grad_block(grads),
                pl.BlockSpec((fours, 1, rows, heads), lambda x, high: (0, x, 0, 0)),
            ],
            out_specs=[pl.BlockSpec((tokens, heads), lambda x, high: (0, 0))] * 2,
            scratch_shapes=[pltpu.VMEM((2, tokens, heads), jnp.float32)],
        ),
        out_shape=[out, out],
        compiler_params=pltpu.CompilerParams(vmem_limit_bytes=VMEM_LIMIT),
        cost_estimate=pl.CostEstimate(
            flops=2 * grads.size * heads,
            bytes_accessed=2 * (grads.size + weights.size),
            transcendentals=0,
        ),
    )(high, grads, weights)


def swap_y(array, target):
    pairs = []
    for low in range(2):
        for high in range(2):
            to_low, to_high = target(low, high)
            pairs.append((low * 2 + high, to_low * 2 + to_high))
    return lax.ppermute(array, ("yl", "yh"), pairs)


def turned(array):
    return swap_y(array, lambda low, high: (high, low))


def along(array, step):
    return lax.ppermute(array, Z, [(z, (z + step) % 16) for z in range(16)])


def gather_rows(own_rows):
    column = lax.all_gather(own_rows, "za", axis=0)
    before = along(column, 1)
    after = along(column, -1)
    far = jnp.concatenate([along(column[:2], 2), along(column[2:], -2)])
    blocks = [column, after, far, before]
    shift = (4 - lax.axis_index("zb")) % 4
    return lax.dynamic_slice_in_dim(jnp.stack(blocks + blocks), shift, 4, axis=0)


def sum_over(array, axis, count):
    spread = lax.all_to_all(jnp.broadcast_to(array[None], (count,) + array.shape), axis, 0, 0)
    return jnp.sum(spread, axis=0)


def per_device(queries_raw, keys_raw, values, grad_out, out_weight, norm_gains):
    high = lax.axis_index("yh").reshape(1)
    grads = lax.all_gather(grad_out, ("yl", "x", "c"), axis=0)
    grads = grads.reshape((2, 4, 2) + grad_out.shape)

    attn = forward(queries_raw, keys_raw, values, norm_gains)
    attn_same = turned(attn)
    attn_other = swap_y(attn, lambda low, up: (up, 1 - low))
    own_rows, attn_same = lax.optimization_barrier((turned(out_weight), attn_same))
    weights = gather_rows(own_rows)
    grads, weights = lax.optimization_barrier((grads, weights))

    wgrad = weight_product(high, grads, attn_same, attn_other)
    shard = lax.psum_scatter(wgrad, Z, scatter_dimension=0, tiled=True)

    weights, _ = lax.optimization_barrier((weights, wgrad))
    part_same, part_other = token_product(high, grads, weights)
    came_same = turned(part_same)
    came_other = swap_y(part_other, lambda low, up: (1 - up, low))
    queries_grad, keys_grad, values_grad, terms = backward(
        queries_raw, keys_raw, values, came_same, came_other, norm_gains
    )
    gains_grad = sum_over(sum_over(terms, ("yl", "yh", "x", "c"), 32), Z, 16)
    shard, gains_grad = lax.optimization_barrier((shard, gains_grad))
    weight_grad = turned(shard).astype(jnp.float32)
    return (queries_grad, keys_grad, values_grad, weight_grad, gains_grad)


def solution(mesh):
    fine = Mesh(mesh.devices.reshape(SIZES), AXES)
    spec = P(("yl", "za", "zb"), ("yh", "x", "c"))
    return jax.shard_map(
        per_device,
        mesh=fine,
        in_specs=(spec, spec, spec, spec, spec, P()),
        out_specs=(spec, spec, spec, spec, P()),
        check_vma=False,
    )
```

```python
import jax
import jax.numpy as jnp
from jax import lax
from jax.experimental import pallas as pl
from jax.experimental.pallas import tpu as pltpu
from jax.sharding import Mesh, PartitionSpec as P

HD = 128
PATCH = 256
EPSILON = 1e-06
SCALE = HD ** (-0.5)
AXES = ("yl", "za", "zb", "yh", "x", "c")
SIZES = (2, 4, 4, 2, 4, 2)
Z = ("za", "zb")
VMEM_LIMIT = 56 * 1024 * 1024


def normalize(raw, gain):
    values32 = raw.astype(jnp.float32)
    center = values32 - jnp.mean(values32, axis=-1, keepdims=True)
    inverse = lax.rsqrt(jnp.mean(center * center, axis=-1, keepdims=True) + EPSILON)
    unit = center * inverse
    return (unit, inverse, (unit * gain).astype(jnp.bfloat16))


def unnormalize(grad, unit, inverse, gain):
    scaled = grad * gain
    centered = scaled - jnp.mean(scaled, axis=-1, keepdims=True)
    return (centered - unit * jnp.mean(scaled * unit, axis=-1, keepdims=True)) * inverse


def product(left, right, left_dim, right_dim):
    return lax.dot_general(
        left, right, (((left_dim,), (right_dim,)), ((), ())), preferred_element_type=jnp.float32
    )


def softmax(q_norm, k_norm):
    scores = product(q_norm, k_norm, 1, 1) * SCALE
    expo = jnp.exp(scores - jnp.max(scores, axis=-1, keepdims=True))
    return expo / jnp.sum(expo, axis=-1, keepdims=True)


def forward_kernel(q_ref, k_ref, v_ref, gains_ref, attn_ref):
    for head in range(q_ref.shape[1] // HD):
        cols = slice(head * HD, (head + 1) * HD)
        _, _, q_norm = normalize(q_ref[:, cols], gains_ref[0:1, :])
        _, _, k_norm = normalize(k_ref[:, cols], gains_ref[1:2, :])
        prob_low = softmax(q_norm, k_norm).astype(jnp.bfloat16)
        attn_ref[:, cols] = product(prob_low, v_ref[:, cols], 1, 0).astype(jnp.bfloat16)


def forward(queries_raw, keys_raw, values, norm_gains):
    tokens, width = queries_raw.shape
    block = pl.BlockSpec((PATCH, width), lambda i: (i, 0))
    return pl.pallas_call(
        forward_kernel,
        grid=(tokens // PATCH,),
        in_specs=[block, block, block, pl.BlockSpec((2, HD), lambda i: (0, 0))],
        out_specs=block,
        out_shape=jax.ShapeDtypeStruct((tokens, width), jnp.bfloat16),
        compiler_params=pltpu.CompilerParams(vmem_limit_bytes=VMEM_LIMIT),
    )(queries_raw, keys_raw, values, norm_gains)


def backward_kernel(
    q_ref, k_ref, v_ref, one_ref, two_ref, gains_ref, qg_ref, kg_ref, vg_ref, terms_ref
):
    @pl.when(pl.program_id(0) == 0)
    def _():
        terms_ref[...] = jnp.zeros_like(terms_ref)

    q_gain, k_gain = gains_ref[0:1, :], gains_ref[1:2, :]
    for head in range(q_ref.shape[1] // HD):
        cols = slice(head * HD, (head + 1) * HD)
        value = v_ref[:, cols]
        q_unit, q_inverse, q_norm = normalize(q_ref[:, cols], q_gain)
        k_unit, k_inverse, k_norm = normalize(k_ref[:, cols], k_gain)
        prob = softmax(q_norm, k_norm)
        prob_low = prob.astype(jnp.bfloat16)
        attn = product(prob_low, value, 1, 0).astype(jnp.bfloat16)
        grad = one_ref[:, cols].astype(jnp.float32) + two_ref[:, cols].astype(jnp.float32)
        grad = grad.astype(jnp.bfloat16)
        vg_ref[:, cols] = product(prob_low, grad, 0, 0).astype(jnp.bfloat16)
        delta = jnp.sum(
            grad.astype(jnp.float32) * attn.astype(jnp.float32), axis=-1, keepdims=True
        )
        score_grad = (prob * (product(grad, value, 1, 1) - delta)).astype(jnp.bfloat16)
        qn_grad = product(score_grad, k_norm, 1, 0) * SCALE
        kn_grad = product(score_grad, q_norm, 0, 0) * SCALE
        terms_ref[0:1, :] += jnp.sum(qn_grad * q_unit, axis=0, keepdims=True)
        terms_ref[1:2, :] += jnp.sum(kn_grad * k_unit, axis=0, keepdims=True)
        qg_ref[:, cols] = unnormalize(qn_grad, q_unit, q_inverse, q_gain).astype(jnp.bfloat16)
        kg_ref[:, cols] = unnormalize(kn_grad, k_unit, k_inverse, k_gain).astype(jnp.bfloat16)


def backward(queries_raw, keys_raw, values, part_one, part_two, norm_gains):
    tokens, width = queries_raw.shape
    block = pl.BlockSpec((PATCH, width), lambda i: (i, 0))
    gains = pl.BlockSpec((2, HD), lambda i: (0, 0))
    out = jax.ShapeDtypeStruct((tokens, width), jnp.bfloat16)
    return pl.pallas_call(
        backward_kernel,
        grid=(tokens // PATCH,),
        in_specs=[block] * 5 + [gains],
        out_specs=[block, block, block, gains],
        out_shape=[out, out, out, jax.ShapeDtypeStruct((2, HD), jnp.float32)],
        compiler_params=pltpu.CompilerParams(vmem_limit_bytes=VMEM_LIMIT),
    )(queries_raw, keys_raw, values, part_one, part_two, norm_gains)


def weight_kernel(high_ref, grad_ref, same_ref, other_ref, wgrad_ref):
    high = high_ref[0]
    width = grad_ref.shape[4]
    for core in range(2):
        term = product(grad_ref[high, 0, core], same_ref[...], 0, 0)
        term += product(grad_ref[1 - high, 0, core], other_ref[...], 0, 0)
        wgrad_ref[core * width : (core + 1) * width] = term.astype(wgrad_ref.dtype)


def grad_block(grads):
    return pl.BlockSpec((2, 1) + grads.shape[2:], lambda x, high: (0, x, 0, 0, 0))


def weight_product(high, grads, attn_same, attn_other):
    _, blocks, cores, tokens, width = grads.shape
    heads = attn_same.shape[1]
    attn = pl.BlockSpec((tokens, heads), lambda x, high: (0, 0))
    return pl.pallas_call(
        weight_kernel,
        grid_spec=pltpu.PrefetchScalarGridSpec(
            num_scalar_prefetch=1,
            grid=(blocks,),
            in_specs=[grad_block(grads), attn, attn],
            out_specs=pl.BlockSpec((cores * width, heads), lambda x, high: (x, 0)),
        ),
        out_shape=jax.ShapeDtypeStruct((blocks * cores * width, heads), jnp.bfloat16),
        compiler_params=pltpu.CompilerParams(vmem_limit_bytes=VMEM_LIMIT),
        cost_estimate=pl.CostEstimate(
            flops=2 * grads.size * heads,
            bytes_accessed=2 * (grads.size + blocks * cores * width * heads),
            transcendentals=0,
        ),
    )(high, grads, attn_same, attn_other)


def token_kernel(high_ref, grad_ref, weight_ref, same_ref, other_ref, total):
    step = pl.program_id(0)
    high = high_ref[0]
    weights = weight_ref[...].reshape(-1, weight_ref.shape[3])
    width = grad_ref.shape[4]

    @pl.when(step == 0)
    def _():
        total[...] = jnp.zeros_like(total)

    for index, low in enumerate((high, 1 - high)):
        term = product(grad_ref[low, 0, 0], weights[:width], 1, 0)
        total[index] += term + product(grad_ref[low, 0, 1], weights[width:], 1, 0)

    @pl.when(step == pl.num_programs(0) - 1)
    def _():
        same_ref[...] = total[0].astype(same_ref.dtype)
        other_ref[...] = total[1].astype(other_ref.dtype)


def token_product(high, grads, weights):
    _, blocks, _, tokens, _ = grads.shape
    fours, _, rows, heads = weights.shape
    out = jax.ShapeDtypeStruct((tokens, heads), jnp.bfloat16)
    return pl.pallas_call(
        token_kernel,
        grid_spec=pltpu.PrefetchScalarGridSpec(
            num_scalar_prefetch=1,
            grid=(blocks,),
            in_specs=[
                grad_block(grads),
                pl.BlockSpec((fours, 1, rows, heads), lambda x, high: (0, x, 0, 0)),
            ],
            out_specs=[pl.BlockSpec((tokens, heads), lambda x, high: (0, 0))] * 2,
            scratch_shapes=[pltpu.VMEM((2, tokens, heads), jnp.float32)],
        ),
        out_shape=[out, out],
        compiler_params=pltpu.CompilerParams(vmem_limit_bytes=VMEM_LIMIT),
        cost_estimate=pl.CostEstimate(
            flops=2 * grads.size * heads,
            bytes_accessed=2 * (grads.size + weights.size),
            transcendentals=0,
        ),
    )(high, grads, weights)


def swap_y(array, target):
    pairs = []
    for low in range(2):
        for high in range(2):
            to_low, to_high = target(low, high)
            pairs.append((low * 2 + high, to_low * 2 + to_high))
    return lax.ppermute(array, ("yl", "yh"), pairs)


def turned(array):
    return swap_y(array, lambda low, high: (high, low))


def along(array, step):
    return lax.ppermute(array, Z, [(z, (z + step) % 16) for z in range(16)])


def gather_rows(own_rows):
    column = lax.all_gather(own_rows, "za", axis=0)
    before = along(column, 1)
    after = along(column, -1)
    far = jnp.concatenate([along(column[:2], 2), along(column[2:], -2)])
    blocks = [column, after, far, before]
    shift = (4 - lax.axis_index("zb")) % 4
    return lax.dynamic_slice_in_dim(jnp.stack(blocks + blocks), shift, 4, axis=0)


def sum_over(array, axis, count):
    spread = lax.all_to_all(jnp.broadcast_to(array[None], (count,) + array.shape), axis, 0, 0)
    return jnp.sum(spread, axis=0)


def per_device(queries_raw, keys_raw, values, grad_out, out_weight, norm_gains):
    high = lax.axis_index("yh").reshape(1)
    grads = lax.all_gather(grad_out, ("yl", "x", "c"), axis=0)
    grads = grads.reshape((2, 4, 2) + grad_out.shape)

    attn = forward(queries_raw, keys_raw, values, norm_gains)
    attn_same = turned(attn)
    attn_other = swap_y(attn, lambda low, up: (up, 1 - low))
    own_rows, attn_other = lax.optimization_barrier((turned(out_weight), attn_other))
    weights = gather_rows(own_rows)
    grads, weights = lax.optimization_barrier((grads, weights))

    wgrad = weight_product(high, grads, attn_same, attn_other)
    shard = lax.psum_scatter(wgrad, Z, scatter_dimension=0, tiled=True)

    weights, _ = lax.optimization_barrier((weights, wgrad))
    part_same, part_other = token_product(high, grads, weights)
    came_same = turned(part_same)
    came_other = swap_y(part_other, lambda low, up: (1 - up, low))
    queries_grad, keys_grad, values_grad, terms = backward(
        queries_raw, keys_raw, values, came_same, came_other, norm_gains
    )
    gains_grad = sum_over(sum_over(terms, ("yl", "yh", "x", "c"), 32), Z, 16)
    shard, gains_grad = lax.optimization_barrier((shard, gains_grad))
    weight_grad = turned(shard).astype(jnp.float32)
    return (queries_grad, keys_grad, values_grad, weight_grad, gains_grad)


def solution(mesh):
    fine = Mesh(mesh.devices.reshape(SIZES), AXES)
    spec = P(("yl", "za", "zb"), ("yh", "x", "c"))
    return jax.shard_map(
        per_device,
        mesh=fine,
        in_specs=(spec, spec, spec, spec, spec, P()),
        out_specs=(spec, spec, spec, spec, P()),
        check_vma=False,
    )
```

```python
import jax
import jax.numpy as jnp
from jax import lax
from jax.experimental import pallas as pl
from jax.experimental.pallas import tpu as pltpu
from jax.sharding import Mesh, PartitionSpec as P

HD = 128
PATCH = 256
EPSILON = 1e-06
SCALE = HD ** (-0.5)
AXES = ("yl", "za", "zb", "yh", "x", "c")
SIZES = (2, 4, 4, 2, 4, 2)
Z = ("za", "zb")
VMEM_LIMIT = 56 * 1024 * 1024


def normalize(raw, gain):
    values32 = raw.astype(jnp.float32)
    center = values32 - jnp.mean(values32, axis=-1, keepdims=True)
    inverse = lax.rsqrt(jnp.mean(center * center, axis=-1, keepdims=True) + EPSILON)
    unit = center * inverse
    return (unit, inverse, (unit * gain).astype(jnp.bfloat16))


def unnormalize(grad, unit, inverse, gain):
    scaled = grad * gain
    centered = scaled - jnp.mean(scaled, axis=-1, keepdims=True)
    return (centered - unit * jnp.mean(scaled * unit, axis=-1, keepdims=True)) * inverse


def product(left, right, left_dim, right_dim):
    return lax.dot_general(
        left, right, (((left_dim,), (right_dim,)), ((), ())), preferred_element_type=jnp.float32
    )


def softmax(q_norm, k_norm):
    scores = product(q_norm, k_norm, 1, 1) * SCALE
    expo = jnp.exp(scores - jnp.max(scores, axis=-1, keepdims=True))
    return expo / jnp.sum(expo, axis=-1, keepdims=True)


def forward_kernel(q_ref, k_ref, v_ref, gains_ref, attn_ref):
    for head in range(q_ref.shape[1] // HD):
        cols = slice(head * HD, (head + 1) * HD)
        _, _, q_norm = normalize(q_ref[:, cols], gains_ref[0:1, :])
        _, _, k_norm = normalize(k_ref[:, cols], gains_ref[1:2, :])
        prob_low = softmax(q_norm, k_norm).astype(jnp.bfloat16)
        attn_ref[:, cols] = product(prob_low, v_ref[:, cols], 1, 0).astype(jnp.bfloat16)


def forward(queries_raw, keys_raw, values, norm_gains):
    tokens, width = queries_raw.shape
    block = pl.BlockSpec((PATCH, width), lambda i: (i, 0))
    return pl.pallas_call(
        forward_kernel,
        grid=(tokens // PATCH,),
        in_specs=[block, block, block, pl.BlockSpec((2, HD), lambda i: (0, 0))],
        out_specs=block,
        out_shape=jax.ShapeDtypeStruct((tokens, width), jnp.bfloat16),
        compiler_params=pltpu.CompilerParams(vmem_limit_bytes=VMEM_LIMIT),
    )(queries_raw, keys_raw, values, norm_gains)


def backward_kernel(
    q_ref, k_ref, v_ref, one_ref, two_ref, gains_ref, qg_ref, kg_ref, vg_ref, terms_ref
):
    @pl.when(pl.program_id(0) == 0)
    def _():
        terms_ref[...] = jnp.zeros_like(terms_ref)

    q_gain, k_gain = gains_ref[0:1, :], gains_ref[1:2, :]
    for head in range(q_ref.shape[1] // HD):
        cols = slice(head * HD, (head + 1) * HD)
        value = v_ref[:, cols]
        q_unit, q_inverse, q_norm = normalize(q_ref[:, cols], q_gain)
        k_unit, k_inverse, k_norm = normalize(k_ref[:, cols], k_gain)
        prob = softmax(q_norm, k_norm)
        prob_low = prob.astype(jnp.bfloat16)
        attn = product(prob_low, value, 1, 0).astype(jnp.bfloat16)
        grad = one_ref[:, cols].astype(jnp.float32) + two_ref[:, cols].astype(jnp.float32)
        grad = grad.astype(jnp.bfloat16)
        vg_ref[:, cols] = product(prob_low, grad, 0, 0).astype(jnp.bfloat16)
        delta = jnp.sum(
            grad.astype(jnp.float32) * attn.astype(jnp.float32), axis=-1, keepdims=True
        )
        score_grad = (prob * (product(grad, value, 1, 1) - delta)).astype(jnp.bfloat16)
        qn_grad = product(score_grad, k_norm, 1, 0) * SCALE
        kn_grad = product(score_grad, q_norm, 0, 0) * SCALE
        terms_ref[0:1, :] += jnp.sum(qn_grad * q_unit, axis=0, keepdims=True)
        terms_ref[1:2, :] += jnp.sum(kn_grad * k_unit, axis=0, keepdims=True)
        qg_ref[:, cols] = unnormalize(qn_grad, q_unit, q_inverse, q_gain).astype(jnp.bfloat16)
        kg_ref[:, cols] = unnormalize(kn_grad, k_unit, k_inverse, k_gain).astype(jnp.bfloat16)


def backward(queries_raw, keys_raw, values, part_one, part_two, norm_gains):
    tokens, width = queries_raw.shape
    block = pl.BlockSpec((PATCH, width), lambda i: (i, 0))
    gains = pl.BlockSpec((2, HD), lambda i: (0, 0))
    out = jax.ShapeDtypeStruct((tokens, width), jnp.bfloat16)
    return pl.pallas_call(
        backward_kernel,
        grid=(tokens // PATCH,),
        in_specs=[block] * 5 + [gains],
        out_specs=[block, block, block, gains],
        out_shape=[out, out, out, jax.ShapeDtypeStruct((2, HD), jnp.float32)],
        compiler_params=pltpu.CompilerParams(vmem_limit_bytes=VMEM_LIMIT),
    )(queries_raw, keys_raw, values, part_one, part_two, norm_gains)


def weight_kernel(high_ref, grad_ref, same_ref, other_ref, wgrad_ref):
    high = high_ref[0]
    width = grad_ref.shape[4]
    for core in range(2):
        term = product(grad_ref[high, 0, core], same_ref[...], 0, 0)
        term += product(grad_ref[1 - high, 0, core], other_ref[...], 0, 0)
        wgrad_ref[core * width : (core + 1) * width] = term.astype(wgrad_ref.dtype)


def grad_block(grads):
    return pl.BlockSpec((2, 1) + grads.shape[2:], lambda x, high: (0, x, 0, 0, 0))


def weight_product(high, grads, attn_same, attn_other):
    _, blocks, cores, tokens, width = grads.shape
    heads = attn_same.shape[1]
    attn = pl.BlockSpec((tokens, heads), lambda x, high: (0, 0))
    return pl.pallas_call(
        weight_kernel,
        grid_spec=pltpu.PrefetchScalarGridSpec(
            num_scalar_prefetch=1,
            grid=(blocks,),
            in_specs=[grad_block(grads), attn, attn],
            out_specs=pl.BlockSpec((cores * width, heads), lambda x, high: (x, 0)),
        ),
        out_shape=jax.ShapeDtypeStruct((blocks * cores * width, heads), jnp.bfloat16),
        compiler_params=pltpu.CompilerParams(vmem_limit_bytes=VMEM_LIMIT),
        cost_estimate=pl.CostEstimate(
            flops=2 * grads.size * heads,
            bytes_accessed=2 * (grads.size + blocks * cores * width * heads),
            transcendentals=0,
        ),
    )(high, grads, attn_same, attn_other)


def token_kernel(high_ref, grad_ref, weight_ref, same_ref, other_ref, total):
    step = pl.program_id(0)
    high = high_ref[0]
    weights = weight_ref[...].reshape(-1, weight_ref.shape[3])
    width = grad_ref.shape[4]

    @pl.when(step == 0)
    def _():
        total[...] = jnp.zeros_like(total)

    for index, low in enumerate((high, 1 - high)):
        term = product(grad_ref[low, 0, 0], weights[:width], 1, 0)
        total[index] += term + product(grad_ref[low, 0, 1], weights[width:], 1, 0)

    @pl.when(step == pl.num_programs(0) - 1)
    def _():
        same_ref[...] = total[0].astype(same_ref.dtype)
        other_ref[...] = total[1].astype(other_ref.dtype)


def token_product(high, grads, weights):
    _, blocks, _, tokens, _ = grads.shape
    fours, _, rows, heads = weights.shape
    out = jax.ShapeDtypeStruct((tokens, heads), jnp.bfloat16)
    return pl.pallas_call(
        token_kernel,
        grid_spec=pltpu.PrefetchScalarGridSpec(
            num_scalar_prefetch=1,
            grid=(blocks,),
            in_specs=[
                grad_block(grads),
                pl.BlockSpec((fours, 1, rows, heads), lambda x, high: (0, x, 0, 0)),
            ],
            out_specs=[pl.BlockSpec((tokens, heads), lambda x, high: (0, 0))] * 2,
            scratch_shapes=[pltpu.VMEM((2, tokens, heads), jnp.float32)],
        ),
        out_shape=[out, out],
        compiler_params=pltpu.CompilerParams(vmem_limit_bytes=VMEM_LIMIT),
        cost_estimate=pl.CostEstimate(
            flops=2 * grads.size * heads,
            bytes_accessed=2 * (grads.size + weights.size),
            transcendentals=0,
        ),
    )(high, grads, weights)


def swap_y(array, target):
    pairs = []
    for low in range(2):
        for high in range(2):
            to_low, to_high = target(low, high)
            pairs.append((low * 2 + high, to_low * 2 + to_high))
    return lax.ppermute(array, ("yl", "yh"), pairs)


def turned(array):
    return swap_y(array, lambda low, high: (high, low))


def along(array, step):
    return lax.ppermute(array, Z, [(z, (z + step) % 16) for z in range(16)])


def gather_rows(own_rows):
    column = lax.all_gather(own_rows, "za", axis=0)
    before = along(column, 1)
    after = along(column, -1)
    far = jnp.concatenate([along(column[:2], 2), along(column[2:], -2)])
    blocks = [column, after, far, before]
    shift = (4 - lax.axis_index("zb")) % 4
    rows = lax.dynamic_slice_in_dim(jnp.stack(blocks + blocks), shift, 4, axis=0)
    return rows, before, after


def sum_over(array, axis, count):
    spread = lax.all_to_all(jnp.broadcast_to(array[None], (count,) + array.shape), axis, 0, 0)
    return jnp.sum(spread, axis=0)


def per_device(queries_raw, keys_raw, values, grad_out, out_weight, norm_gains):
    high = lax.axis_index("yh").reshape(1)
    grads = lax.all_gather(grad_out, ("yl", "x", "c"), axis=0)
    grads = grads.reshape((2, 4, 2) + grad_out.shape)

    attn = forward(queries_raw, keys_raw, values, norm_gains)
    attn_same = turned(attn)
    attn_other = swap_y(attn, lambda low, up: (up, 1 - low))
    own_rows, attn_other = lax.optimization_barrier((turned(out_weight), attn_other))
    weights, before, after = gather_rows(own_rows)
    grads, _, _ = lax.optimization_barrier((grads, before, after))

    wgrad = weight_product(high, grads, attn_same, attn_other)
    shard = lax.psum_scatter(wgrad, Z, scatter_dimension=0, tiled=True)

    weights, _ = lax.optimization_barrier((weights, wgrad))
    part_same, part_other = token_product(high, grads, weights)
    came_same = turned(part_same)
    came_other = swap_y(part_other, lambda low, up: (1 - up, low))
    queries_grad, keys_grad, values_grad, terms = backward(
        queries_raw, keys_raw, values, came_same, came_other, norm_gains
    )
    gains_grad = sum_over(sum_over(terms, ("yl", "yh", "x", "c"), 32), Z, 16)
    shard, gains_grad = lax.optimization_barrier((shard, gains_grad))
    weight_grad = turned(shard).astype(jnp.float32)
    return (queries_grad, keys_grad, values_grad, weight_grad, gains_grad)


def solution(mesh):
    fine = Mesh(mesh.devices.reshape(SIZES), AXES)
    spec = P(("yl", "za", "zb"), ("yh", "x", "c"))
    return jax.shard_map(
        per_device,
        mesh=fine,
        in_specs=(spec, spec, spec, spec, spec, P()),
        out_specs=(spec, spec, spec, spec, P()),
        check_vma=False,
    )
```

```python
import jax
import jax.numpy as jnp
from jax import lax
from jax.experimental import pallas as pl
from jax.experimental.pallas import tpu as pltpu
from jax.sharding import Mesh, PartitionSpec as P

HD = 128
PATCH = 256
EPSILON = 1e-06
SCALE = HD ** (-0.5)
AXES = ("yl", "za", "zm", "zl", "yh", "x", "c")
SIZES = (2, 4, 2, 2, 2, 4, 2)
Z = ("za", "zm", "zl")
VMEM_LIMIT = 56 * 1024 * 1024


def normalize(raw, gain):
    values32 = raw.astype(jnp.float32)
    center = values32 - jnp.mean(values32, axis=-1, keepdims=True)
    inverse = lax.rsqrt(jnp.mean(center * center, axis=-1, keepdims=True) + EPSILON)
    unit = center * inverse
    return (unit, inverse, (unit * gain).astype(jnp.bfloat16))


def unnormalize(grad, unit, inverse, gain):
    scaled = grad * gain
    centered = scaled - jnp.mean(scaled, axis=-1, keepdims=True)
    return (centered - unit * jnp.mean(scaled * unit, axis=-1, keepdims=True)) * inverse


def product(left, right, left_dim, right_dim):
    return lax.dot_general(
        left, right, (((left_dim,), (right_dim,)), ((), ())), preferred_element_type=jnp.float32
    )


def softmax(q_norm, k_norm):
    scores = product(q_norm, k_norm, 1, 1) * SCALE
    expo = jnp.exp(scores - jnp.max(scores, axis=-1, keepdims=True))
    return expo / jnp.sum(expo, axis=-1, keepdims=True)


def forward_kernel(q_ref, k_ref, v_ref, gains_ref, attn_ref):
    for head in range(q_ref.shape[1] // HD):
        cols = slice(head * HD, (head + 1) * HD)
        _, _, q_norm = normalize(q_ref[:, cols], gains_ref[0:1, :])
        _, _, k_norm = normalize(k_ref[:, cols], gains_ref[1:2, :])
        prob_low = softmax(q_norm, k_norm).astype(jnp.bfloat16)
        attn_ref[:, cols] = product(prob_low, v_ref[:, cols], 1, 0).astype(jnp.bfloat16)


def forward(queries_raw, keys_raw, values, norm_gains):
    tokens, width = queries_raw.shape
    block = pl.BlockSpec((PATCH, width), lambda i: (i, 0))
    return pl.pallas_call(
        forward_kernel,
        grid=(tokens // PATCH,),
        in_specs=[block, block, block, pl.BlockSpec((2, HD), lambda i: (0, 0))],
        out_specs=block,
        out_shape=jax.ShapeDtypeStruct((tokens, width), jnp.bfloat16),
        compiler_params=pltpu.CompilerParams(vmem_limit_bytes=VMEM_LIMIT),
    )(queries_raw, keys_raw, values, norm_gains)


def backward_kernel(
    q_ref, k_ref, v_ref, one_ref, two_ref, gains_ref, qg_ref, kg_ref, vg_ref, terms_ref
):
    @pl.when(pl.program_id(0) == 0)
    def _():
        terms_ref[...] = jnp.zeros_like(terms_ref)

    q_gain, k_gain = gains_ref[0:1, :], gains_ref[1:2, :]
    for head in range(q_ref.shape[1] // HD):
        cols = slice(head * HD, (head + 1) * HD)
        value = v_ref[:, cols]
        q_unit, q_inverse, q_norm = normalize(q_ref[:, cols], q_gain)
        k_unit, k_inverse, k_norm = normalize(k_ref[:, cols], k_gain)
        prob = softmax(q_norm, k_norm)
        prob_low = prob.astype(jnp.bfloat16)
        attn = product(prob_low, value, 1, 0).astype(jnp.bfloat16)
        grad = one_ref[:, cols].astype(jnp.float32) + two_ref[:, cols].astype(jnp.float32)
        grad = grad.astype(jnp.bfloat16)
        vg_ref[:, cols] = product(prob_low, grad, 0, 0).astype(jnp.bfloat16)
        delta = jnp.sum(
            grad.astype(jnp.float32) * attn.astype(jnp.float32), axis=-1, keepdims=True
        )
        score_grad = (prob * (product(grad, value, 1, 1) - delta)).astype(jnp.bfloat16)
        qn_grad = product(score_grad, k_norm, 1, 0) * SCALE
        kn_grad = product(score_grad, q_norm, 0, 0) * SCALE
        terms_ref[0:1, :] += jnp.sum(qn_grad * q_unit, axis=0, keepdims=True)
        terms_ref[1:2, :] += jnp.sum(kn_grad * k_unit, axis=0, keepdims=True)
        qg_ref[:, cols] = unnormalize(qn_grad, q_unit, q_inverse, q_gain).astype(jnp.bfloat16)
        kg_ref[:, cols] = unnormalize(kn_grad, k_unit, k_inverse, k_gain).astype(jnp.bfloat16)


def backward(queries_raw, keys_raw, values, part_one, part_two, norm_gains):
    tokens, width = queries_raw.shape
    block = pl.BlockSpec((PATCH, width), lambda i: (i, 0))
    gains = pl.BlockSpec((2, HD), lambda i: (0, 0))
    out = jax.ShapeDtypeStruct((tokens, width), jnp.bfloat16)
    return pl.pallas_call(
        backward_kernel,
        grid=(tokens // PATCH,),
        in_specs=[block] * 5 + [gains],
        out_specs=[block, block, block, gains],
        out_shape=[out, out, out, jax.ShapeDtypeStruct((2, HD), jnp.float32)],
        compiler_params=pltpu.CompilerParams(vmem_limit_bytes=VMEM_LIMIT),
    )(queries_raw, keys_raw, values, part_one, part_two, norm_gains)


def weight_kernel(high_ref, grad_ref, same_ref, other_ref, wgrad_ref):
    high = high_ref[0]
    width = grad_ref.shape[4]
    for core in range(2):
        term = product(grad_ref[high, 0, core], same_ref[...], 0, 0)
        term += product(grad_ref[1 - high, 0, core], other_ref[...], 0, 0)
        wgrad_ref[core * width : (core + 1) * width] = term.astype(wgrad_ref.dtype)


def grad_block(grads):
    return pl.BlockSpec((2, 1) + grads.shape[2:], lambda x, high: (0, x, 0, 0, 0))


def weight_product(high, grads, attn_same, attn_other):
    _, blocks, cores, tokens, width = grads.shape
    heads = attn_same.shape[1]
    attn = pl.BlockSpec((tokens, heads), lambda x, high: (0, 0))
    return pl.pallas_call(
        weight_kernel,
        grid_spec=pltpu.PrefetchScalarGridSpec(
            num_scalar_prefetch=1,
            grid=(blocks,),
            in_specs=[grad_block(grads), attn, attn],
            out_specs=pl.BlockSpec((cores * width, heads), lambda x, high: (x, 0)),
        ),
        out_shape=jax.ShapeDtypeStruct((blocks * cores * width, heads), jnp.bfloat16),
        compiler_params=pltpu.CompilerParams(vmem_limit_bytes=VMEM_LIMIT),
        cost_estimate=pl.CostEstimate(
            flops=2 * grads.size * heads,
            bytes_accessed=2 * (grads.size + blocks * cores * width * heads),
            transcendentals=0,
        ),
    )(high, grads, attn_same, attn_other)


def token_kernel(high_ref, grad_ref, weight_ref, same_ref, other_ref, total):
    step = pl.program_id(0)
    high = high_ref[0]
    width = grad_ref.shape[4]

    @pl.when(step == 0)
    def _():
        total[...] = jnp.zeros_like(total)

    for index, low in enumerate((high, 1 - high)):
        term = product(grad_ref[low, 0, 0], weight_ref[:, 0].reshape(width, -1), 1, 0)
        term += product(grad_ref[low, 0, 1], weight_ref[:, 1].reshape(width, -1), 1, 0)
        total[index] += term

    @pl.when(step == pl.num_programs(0) - 1)
    def _():
        same_ref[...] = total[0].astype(same_ref.dtype)
        other_ref[...] = total[1].astype(other_ref.dtype)


def token_product(high, grads, weights):
    _, blocks, _, tokens, _ = grads.shape
    _, _, rows, heads = weights.shape
    out = jax.ShapeDtypeStruct((tokens, heads), jnp.bfloat16)
    return pl.pallas_call(
        token_kernel,
        grid_spec=pltpu.PrefetchScalarGridSpec(
            num_scalar_prefetch=1,
            grid=(blocks,),
            in_specs=[
                grad_block(grads),
                pl.BlockSpec((2, 2, rows, heads), lambda x, high: (0, x, 0, 0)),
            ],
            out_specs=[pl.BlockSpec((tokens, heads), lambda x, high: (0, 0))] * 2,
            scratch_shapes=[pltpu.VMEM((2, tokens, heads), jnp.float32)],
        ),
        out_shape=[out, out],
        compiler_params=pltpu.CompilerParams(vmem_limit_bytes=VMEM_LIMIT),
        cost_estimate=pl.CostEstimate(
            flops=2 * grads.size * heads,
            bytes_accessed=2 * (grads.size + weights.size),
            transcendentals=0,
        ),
    )(high, grads, weights)


def swap_y(array, target):
    pairs = []
    for low in range(2):
        for high in range(2):
            to_low, to_high = target(low, high)
            pairs.append((low * 2 + high, to_low * 2 + to_high))
    return lax.ppermute(array, ("yl", "yh"), pairs)


def turned(array):
    return swap_y(array, lambda low, high: (high, low))


def along(array, step):
    return lax.ppermute(array, Z, [(z, (z + step) % 16) for z in range(16)])


def gather_rows(own_rows):
    same = lax.all_gather(own_rows, ("za", "zm"), axis=0)
    other = jnp.concatenate([along(same[:4], 1), along(same[4:], -1)])
    blocks = jnp.stack([same, other, same])
    return lax.dynamic_slice_in_dim(blocks, lax.axis_index("zl"), 2, axis=0)


def sum_over(array, axis, count):
    spread = lax.all_to_all(jnp.broadcast_to(array[None], (count,) + array.shape), axis, 0, 0)
    return jnp.sum(spread, axis=0)


def per_device(queries_raw, keys_raw, values, grad_out, out_weight, norm_gains):
    high = lax.axis_index("yh").reshape(1)
    grads = lax.all_gather(grad_out, ("yl", "x", "c"), axis=0)
    grads = grads.reshape((2, 4, 2) + grad_out.shape)

    attn = forward(queries_raw, keys_raw, values, norm_gains)
    attn_same = turned(attn)
    attn_other = swap_y(attn, lambda low, up: (up, 1 - low))
    own_rows, attn_other = lax.optimization_barrier((turned(out_weight), attn_other))
    weights = gather_rows(own_rows)
    grads, weights = lax.optimization_barrier((grads, weights))

    wgrad = weight_product(high, grads, attn_same, attn_other)
    shard = lax.psum_scatter(wgrad, Z, scatter_dimension=0, tiled=True)

    weights, _ = lax.optimization_barrier((weights, wgrad))
    part_same, part_other = token_product(high, grads, weights)
    came_same = turned(part_same)
    came_other = swap_y(part_other, lambda low, up: (1 - up, low))
    queries_grad, keys_grad, values_grad, terms = backward(
        queries_raw, keys_raw, values, came_same, came_other, norm_gains
    )
    gains_grad = sum_over(sum_over(terms, ("yl", "yh", "x", "c"), 32), Z, 16)
    shard, gains_grad = lax.optimization_barrier((shard, gains_grad))
    weight_grad = turned(shard).astype(jnp.float32)
    return (queries_grad, keys_grad, values_grad, weight_grad, gains_grad)


def solution(mesh):
    fine = Mesh(mesh.devices.reshape(SIZES), AXES)
    spec = P(("yl", "za", "zm", "zl"), ("yh", "x", "c"))
    return jax.shard_map(
        per_device,
        mesh=fine,
        in_specs=(spec, spec, spec, spec, spec, P()),
        out_specs=(spec, spec, spec, spec, P()),
        check_vma=False,
    )
```

```python
import jax
import jax.numpy as jnp
from jax import lax
from jax.experimental import pallas as pl
from jax.experimental.pallas import tpu as pltpu
from jax.sharding import Mesh, PartitionSpec as P

HD = 128
PATCH = 256
EPSILON = 1e-06
SCALE = HD ** (-0.5)
AXES = ("yl", "za", "zm", "zl", "yh", "x", "c")
SIZES = (2, 4, 2, 2, 2, 4, 2)
Z = ("za", "zm", "zl")
VMEM_LIMIT = 56 * 1024 * 1024


def normalize(raw, gain):
    values32 = raw.astype(jnp.float32)
    center = values32 - jnp.mean(values32, axis=-1, keepdims=True)
    inverse = lax.rsqrt(jnp.mean(center * center, axis=-1, keepdims=True) + EPSILON)
    unit = center * inverse
    return (unit, inverse, (unit * gain).astype(jnp.bfloat16))


def unnormalize(grad, unit, inverse, gain):
    scaled = grad * gain
    centered = scaled - jnp.mean(scaled, axis=-1, keepdims=True)
    return (centered - unit * jnp.mean(scaled * unit, axis=-1, keepdims=True)) * inverse


def product(left, right, left_dim, right_dim):
    return lax.dot_general(
        left, right, (((left_dim,), (right_dim,)), ((), ())), preferred_element_type=jnp.float32
    )


def softmax(q_norm, k_norm):
    scores = product(q_norm, k_norm, 1, 1) * SCALE
    expo = jnp.exp(scores - jnp.max(scores, axis=-1, keepdims=True))
    return expo / jnp.sum(expo, axis=-1, keepdims=True)


def forward_kernel(q_ref, k_ref, v_ref, gains_ref, attn_ref):
    for head in range(q_ref.shape[1] // HD):
        cols = slice(head * HD, (head + 1) * HD)
        _, _, q_norm = normalize(q_ref[:, cols], gains_ref[0:1, :])
        _, _, k_norm = normalize(k_ref[:, cols], gains_ref[1:2, :])
        prob_low = softmax(q_norm, k_norm).astype(jnp.bfloat16)
        attn_ref[:, cols] = product(prob_low, v_ref[:, cols], 1, 0).astype(jnp.bfloat16)


def forward(queries_raw, keys_raw, values, norm_gains):
    tokens, width = queries_raw.shape
    block = pl.BlockSpec((PATCH, width), lambda i: (i, 0))
    return pl.pallas_call(
        forward_kernel,
        grid=(tokens // PATCH,),
        in_specs=[block, block, block, pl.BlockSpec((2, HD), lambda i: (0, 0))],
        out_specs=block,
        out_shape=jax.ShapeDtypeStruct((tokens, width), jnp.bfloat16),
        compiler_params=pltpu.CompilerParams(vmem_limit_bytes=VMEM_LIMIT),
    )(queries_raw, keys_raw, values, norm_gains)


def backward_kernel(
    q_ref, k_ref, v_ref, one_ref, two_ref, gains_ref, qg_ref, kg_ref, vg_ref, terms_ref
):
    @pl.when(pl.program_id(0) == 0)
    def _():
        terms_ref[...] = jnp.zeros_like(terms_ref)

    q_gain, k_gain = gains_ref[0:1, :], gains_ref[1:2, :]
    for head in range(q_ref.shape[1] // HD):
        cols = slice(head * HD, (head + 1) * HD)
        value = v_ref[:, cols]
        q_unit, q_inverse, q_norm = normalize(q_ref[:, cols], q_gain)
        k_unit, k_inverse, k_norm = normalize(k_ref[:, cols], k_gain)
        prob = softmax(q_norm, k_norm)
        prob_low = prob.astype(jnp.bfloat16)
        attn = product(prob_low, value, 1, 0).astype(jnp.bfloat16)
        grad = one_ref[:, cols].astype(jnp.float32) + two_ref[:, cols].astype(jnp.float32)
        grad = grad.astype(jnp.bfloat16)
        vg_ref[:, cols] = product(prob_low, grad, 0, 0).astype(jnp.bfloat16)
        delta = jnp.sum(
            grad.astype(jnp.float32) * attn.astype(jnp.float32), axis=-1, keepdims=True
        )
        score_grad = (prob * (product(grad, value, 1, 1) - delta)).astype(jnp.bfloat16)
        qn_grad = product(score_grad, k_norm, 1, 0) * SCALE
        kn_grad = product(score_grad, q_norm, 0, 0) * SCALE
        terms_ref[0:1, :] += jnp.sum(qn_grad * q_unit, axis=0, keepdims=True)
        terms_ref[1:2, :] += jnp.sum(kn_grad * k_unit, axis=0, keepdims=True)
        qg_ref[:, cols] = unnormalize(qn_grad, q_unit, q_inverse, q_gain).astype(jnp.bfloat16)
        kg_ref[:, cols] = unnormalize(kn_grad, k_unit, k_inverse, k_gain).astype(jnp.bfloat16)


def backward(queries_raw, keys_raw, values, part_one, part_two, norm_gains):
    tokens, width = queries_raw.shape
    block = pl.BlockSpec((PATCH, width), lambda i: (i, 0))
    gains = pl.BlockSpec((2, HD), lambda i: (0, 0))
    out = jax.ShapeDtypeStruct((tokens, width), jnp.bfloat16)
    return pl.pallas_call(
        backward_kernel,
        grid=(tokens // PATCH,),
        in_specs=[block] * 5 + [gains],
        out_specs=[block, block, block, gains],
        out_shape=[out, out, out, jax.ShapeDtypeStruct((2, HD), jnp.float32)],
        compiler_params=pltpu.CompilerParams(vmem_limit_bytes=VMEM_LIMIT),
    )(queries_raw, keys_raw, values, part_one, part_two, norm_gains)


def weight_kernel(high_ref, grad_ref, same_ref, other_ref, wgrad_ref):
    high = high_ref[0]
    width = grad_ref.shape[4]
    for core in range(2):
        term = product(grad_ref[high, 0, core], same_ref[...], 0, 0)
        term += product(grad_ref[1 - high, 0, core], other_ref[...], 0, 0)
        wgrad_ref[core * width : (core + 1) * width] = term.astype(wgrad_ref.dtype)


def grad_block(grads):
    return pl.BlockSpec((2, 1) + grads.shape[2:], lambda x, high: (0, x, 0, 0, 0))


def weight_product(high, grads, attn_same, attn_other):
    _, blocks, cores, tokens, width = grads.shape
    heads = attn_same.shape[1]
    attn = pl.BlockSpec((tokens, heads), lambda x, high: (0, 0))
    return pl.pallas_call(
        weight_kernel,
        grid_spec=pltpu.PrefetchScalarGridSpec(
            num_scalar_prefetch=1,
            grid=(blocks,),
            in_specs=[grad_block(grads), attn, attn],
            out_specs=pl.BlockSpec((cores * width, heads), lambda x, high: (x, 0)),
        ),
        out_shape=jax.ShapeDtypeStruct((blocks * cores * width, heads), jnp.bfloat16),
        compiler_params=pltpu.CompilerParams(vmem_limit_bytes=VMEM_LIMIT),
        cost_estimate=pl.CostEstimate(
            flops=2 * grads.size * heads,
            bytes_accessed=2 * (grads.size + blocks * cores * width * heads),
            transcendentals=0,
        ),
    )(high, grads, attn_same, attn_other)


def token_kernel(high_ref, grad_ref, weight_ref, same_ref, other_ref, total):
    step = pl.program_id(0)
    high = high_ref[0]
    width = grad_ref.shape[4]

    @pl.when(step == 0)
    def _():
        total[...] = jnp.zeros_like(total)

    for index, low in enumerate((high, 1 - high)):
        term = product(grad_ref[low, 0, 0], weight_ref[:, 0].reshape(width, -1), 1, 0)
        term += product(grad_ref[low, 0, 1], weight_ref[:, 1].reshape(width, -1), 1, 0)
        total[index] += term

    @pl.when(step == pl.num_programs(0) - 1)
    def _():
        same_ref[...] = total[0].astype(same_ref.dtype)
        other_ref[...] = total[1].astype(other_ref.dtype)


def token_product(high, grads, weights):
    _, blocks, _, tokens, _ = grads.shape
    _, _, rows, heads = weights.shape
    out = jax.ShapeDtypeStruct((tokens, heads), jnp.bfloat16)
    return pl.pallas_call(
        token_kernel,
        grid_spec=pltpu.PrefetchScalarGridSpec(
            num_scalar_prefetch=1,
            grid=(blocks,),
            in_specs=[
                grad_block(grads),
                pl.BlockSpec((2, 2, rows, heads), lambda x, high: (0, x, 0, 0)),
            ],
            out_specs=[pl.BlockSpec((tokens, heads), lambda x, high: (0, 0))] * 2,
            scratch_shapes=[pltpu.VMEM((2, tokens, heads), jnp.float32)],
        ),
        out_shape=[out, out],
        compiler_params=pltpu.CompilerParams(vmem_limit_bytes=VMEM_LIMIT),
        cost_estimate=pl.CostEstimate(
            flops=2 * grads.size * heads,
            bytes_accessed=2 * (grads.size + weights.size),
            transcendentals=0,
        ),
    )(high, grads, weights)


def swap_y(array, target):
    pairs = []
    for low in range(2):
        for high in range(2):
            to_low, to_high = target(low, high)
            pairs.append((low * 2 + high, to_low * 2 + to_high))
    return lax.ppermute(array, ("yl", "yh"), pairs)


def turned(array):
    return swap_y(array, lambda low, high: (high, low))


def along(array, step):
    return lax.ppermute(array, Z, [(z, (z + step) % 16) for z in range(16)])


def gather_rows(own_rows):
    same = lax.all_gather(own_rows, ("za", "zm"), axis=0)
    came = along(same[:4], 1), along(same[4:], -1)
    blocks = jnp.stack([same, jnp.concatenate(came), same])
    return lax.dynamic_slice_in_dim(blocks, lax.axis_index("zl"), 2, axis=0), came


def sum_over(array, axis, count):
    spread = lax.all_to_all(jnp.broadcast_to(array[None], (count,) + array.shape), axis, 0, 0)
    return jnp.sum(spread, axis=0)


def per_device(queries_raw, keys_raw, values, grad_out, out_weight, norm_gains):
    high = lax.axis_index("yh").reshape(1)
    grads = lax.all_gather(grad_out, ("yl", "x", "c"), axis=0)
    grads = grads.reshape((2, 4, 2) + grad_out.shape)

    attn = forward(queries_raw, keys_raw, values, norm_gains)
    attn_same = turned(attn)
    attn_other = swap_y(attn, lambda low, up: (up, 1 - low))
    own_rows, attn_other = lax.optimization_barrier((turned(out_weight), attn_other))
    weights, came = gather_rows(own_rows)
    grads, _ = lax.optimization_barrier((grads, came))

    wgrad = weight_product(high, grads, attn_same, attn_other)
    shard = lax.psum_scatter(wgrad, Z, scatter_dimension=0, tiled=True)

    weights, _ = lax.optimization_barrier((weights, wgrad))
    part_same, part_other = token_product(high, grads, weights)
    came_same = turned(part_same)
    came_other = swap_y(part_other, lambda low, up: (1 - up, low))
    queries_grad, keys_grad, values_grad, terms = backward(
        queries_raw, keys_raw, values, came_same, came_other, norm_gains
    )
    gains_grad = sum_over(sum_over(terms, ("yl", "yh", "x", "c"), 32), Z, 16)
    shard, gains_grad = lax.optimization_barrier((shard, gains_grad))
    weight_grad = turned(shard).astype(jnp.float32)
    return (queries_grad, keys_grad, values_grad, weight_grad, gains_grad)


def solution(mesh):
    fine = Mesh(mesh.devices.reshape(SIZES), AXES)
    spec = P(("yl", "za", "zm", "zl"), ("yh", "x", "c"))
    return jax.shard_map(
        per_device,
        mesh=fine,
        in_specs=(spec, spec, spec, spec, spec, P()),
        out_specs=(spec, spec, spec, spec, P()),
        check_vma=False,
    )
```
